512 devices in a mesh: frame: 8 (over y_lo, x), tile: 64 (over y_hi, z, core).
Axes of the slice: x: 4, y: 4 (y_hi: 2, y_lo: 2; y = y_hi * 2 + y_lo), z: 16, core: 2. Of those that a mesh axis runs over, the one named last changes fastest.
Arguments:
- feats: bfloat16 [32, 512, 32, 120], P('frame', 'tile'), may hold values from -6 to 6
- qkv_weight: bfloat16 [2, 120, 720], replicated, may hold values from -0.5 to 0.5
- proj_weight: bfloat16 [2, 240, 120], replicated, may hold values from -0.375 to 0.375
- mlp_in: bfloat16 [2, 120, 480], replicated, may hold values from -0.5 to 0.5
- mlp_out: bfloat16 [2, 240, 120], replicated, may hold values from -0.375 to 0.375
Outputs:
- restored: bfloat16 [32, 512, 32, 120], P('frame', 'tile')
The draws below stay inside these ranges and needn't reach their ends.
All inputs are finite; a program needn't handle non-finite values.
Results may differ from the reference program's by a relative error of at most 0.024.
Values may be sent and summed in bfloat16 or wider, within the bound.
A program may use at most 64 MiB of HBM per device.

```python
import jax
import jax.numpy as jnp
from jax import lax

C = 120
HEADS = 6
WIN = 8
LAYERS = 2
W = 32
HID = 240
FRAMES = 32
HEIGHT = 512


def shard_levels(own_key, extent, cuts, low, largest):
    def one(dim, parts):
        heights = jax.random.uniform(jax.random.fold_in(jax.random.fold_in(own_key, 6), dim), (parts,), jnp.float32, low / len(cuts), largest / len(cuts))
        return jnp.repeat(jnp.exp(heights), extent[dim] // parts).reshape((-1,) + (1,) * (len(extent) - dim - 1))

    level = one(*cuts[0])
    for cut in cuts[1:]:
        level = level * one(*cut)
    return level


def noise(own_key, extent, scale, most, cuts=(), kind=jnp.bfloat16):
    factor_of = shard_levels(own_key, extent, cuts, -0.22, 0.18) if cuts else 1.0
    array = jax.random.normal(own_key, extent, jnp.float32) * scale * factor_of
    return jnp.minimum(jnp.maximum(array, -most), most).astype(kind)


def setup_inputs(seed: int = 0) -> dict:
    streams_of = jax.random.split(jax.random.key(seed), 6)
    feats = noise(streams_of[0], (FRAMES, HEIGHT, W, C), 1.0, 6.0, ((0, 8), (1, 64)))
    qkv_weight = noise(streams_of[1], (LAYERS, C, 6 * C), C ** -0.5, 0.5)
    proj_weight = noise(streams_of[2], (LAYERS, 2 * C, C), (2 * C) ** -0.5, 0.375)
    mlp_in = noise(streams_of[3], (LAYERS, C, 2 * HID), C ** -0.5, 0.5)
    mlp_out = noise(streams_of[4], (LAYERS, HID, C), HID ** -0.5, 0.375)
    return {"feats": feats, "qkv_weight": qkv_weight, "proj_weight": proj_weight, "mlp_in": mlp_in, "mlp_out": mlp_out}


epsilon = 1e-05

def norm_tokens(values):
    center = values - lax.optimization_barrier(jnp.mean(values, -1, keepdims=True))
    spread = lax.optimization_barrier(jnp.mean(center * center, -1, keepdims=True))
    return center * lax.rsqrt(spread + epsilon)

def attend(queries, keys_in, values_in, scaling):
    scores = jnp.einsum('...qd,...kd->...qk', queries.astype(jnp.float32), keys_in.astype(jnp.float32)) * scaling
    powers = jnp.exp(scores)
    softmax_weights = (powers / lax.optimization_barrier(jnp.sum(powers, -1, keepdims=True))).astype(jnp.bfloat16)
    result = jnp.einsum('...qk,...kd->...qd', softmax_weights.astype(jnp.float32), values_in.astype(jnp.float32))
    return result.astype(jnp.bfloat16)

def window_block(windows, qkv_w, proj_w, in_w, out_w):
    number, tokens_in, channels = windows.shape
    head_size = channels // HEADS
    half_tok = tokens_in // 2
    stream = windows.astype(jnp.float32)
    normed = norm_tokens(stream).astype(jnp.bfloat16).reshape(number * tokens_in, channels)
    packed = jnp.dot(normed, qkv_w, preferred_element_type=jnp.float32).astype(jnp.bfloat16)
    packed = packed.reshape(number, tokens_in, 6, HEADS, head_size).transpose(2, 0, 3, 1, 4)
    scaling = head_size ** (-0.5)
    self_part = attend(packed[0], packed[1], packed[2], scaling)
    split_shape = (number, HEADS, 2, half_tok, head_size)
    mutual = attend(packed[3].reshape(split_shape), jnp.flip(packed[4].reshape(split_shape), 2), jnp.flip(packed[5].reshape(split_shape), 2), scaling)
    mutual = mutual.reshape(number, HEADS, tokens_in, head_size)
    joined = jnp.stack([self_part, mutual], 0).transpose(1, 3, 0, 2, 4).reshape(number * tokens_in, 2 * channels)
    summed = stream.reshape(number * tokens_in, channels) + jnp.dot(joined, proj_w, preferred_element_type=jnp.float32)
    middle = summed.astype(jnp.bfloat16)
    normed_two = norm_tokens(middle.astype(jnp.float32)).astype(jnp.bfloat16)
    widened = jnp.dot(normed_two, in_w, preferred_element_type=jnp.float32)
    hidden_units = in_w.shape[1] // 2
    gated_units = (jax.nn.gelu(widened[:, :hidden_units], approximate=False) * widened[:, hidden_units:]).astype(jnp.bfloat16)
    output = middle.astype(jnp.float32) + jnp.dot(gated_units, out_w, preferred_element_type=jnp.float32)
    return output.astype(jnp.bfloat16).reshape(number, tokens_in, channels)

def run_layer(block, qkv_w, proj_w, in_w, out_w):
    frame_count, row_count, col_count, channels = block.shape
    tiles = block.reshape(frame_count // 2, 2, row_count // WIN, WIN, col_count // WIN, WIN, channels)
    tiles = tiles.transpose(0, 2, 4, 1, 3, 5, 6).reshape(frame_count // 2, -1, 2 * WIN * WIN, channels)

    def one_pair(group):
        return window_block(group, qkv_w, proj_w, in_w, out_w)
    finished = lax.map(one_pair, tiles)
    finished = finished.reshape(frame_count // 2, row_count // WIN, col_count // WIN, 2, WIN, WIN, channels)
    return finished.transpose(0, 3, 1, 4, 2, 5, 6).reshape(frame_count, row_count, col_count, channels)

def reference(feats, qkv_weight, proj_weight, mlp_in, mlp_out):
    half_window = WIN // 2
    layer_one = run_layer(feats, qkv_weight[0], proj_weight[0], mlp_in[0], mlp_out[0])
    rolled = jnp.roll(layer_one, (-1, -half_window, -half_window), (0, 1, 2))
    layer_two = run_layer(rolled, qkv_weight[1], proj_weight[1], mlp_in[1], mlp_out[1])
    return jnp.roll(layer_two, (1, half_window, half_window), (0, 1, 2))
```

```python
import functools

import jax
import jax.numpy as jnp
from jax import lax
from jax.experimental import pallas as pl
from jax.experimental.pallas import tpu as pltpu
from jax.sharding import PartitionSpec as P

C, HEADS, HEAD, HID = 120, 6, 20, 240
LANES = 128
EPSILON = 1e-05
LOG2E = 1.4426950408889634
MESH = pl.DeviceIdType.MESH
FIRST_GROUPS = ((0, 4),)
SECOND_GROUPS = ((0, 4),)
BF, F32 = jnp.bfloat16, jnp.float32


def dot(a, b, dims=(((1,), (0,)), ((), ()))):
    return lax.dot_general(a, b, dims, preferred_element_type=F32)


def norm_tokens(x):
    mean = jnp.sum(x, -1, keepdims=True) * (1.0 / C)
    lane = lax.broadcasted_iota(jnp.int32, x.shape, 1)
    center = jnp.where(lane < C, x - mean, 0.0)
    spread = jnp.sum(center * center, -1, keepdims=True) * (1.0 / C)
    return (center * lax.rsqrt(spread + EPSILON)).astype(BF)


def gelu(g):
    return g * 0.5 * (1.0 + lax.erf(g * 0.7071067811865476))


def attend(q, k, v, key_masks, value_masks, ones):
    kb = jnp.concatenate([jnp.where(m, k, jnp.zeros_like(k)) for m in key_masks], 0)
    weights = jnp.exp2(dot(q, kb, (((1,), (1,)), ((), ())))).astype(BF)
    vb = jnp.concatenate([jnp.where(m, v, jnp.zeros_like(v)) for m in value_masks], 0)
    both = dot(weights, jnp.concatenate([vb, ones], 1))
    return both[:, :LANES] * (pl.reciprocal(both[:, LANES:], approx=False) * 16.0)


def layer(x, qkv_w, proj_w, in_w, out_w, ones):
    tokens = x.shape[0]
    packed = dot(norm_tokens(x), qkv_w)
    scaling = HEAD**-0.5 * LOG2E
    lane = lax.broadcasted_iota(jnp.int32, (tokens, LANES), 1)
    row = lax.broadcasted_iota(jnp.int32, (tokens, LANES), 0)
    hit = lane == C + lax.rem(row // 64, 2)
    self_q = (packed[:, 0:128] * scaling).astype(BF)
    self_k = packed[:, 128:256].astype(BF)
    self_v = (packed[:, 256:384] * 2.0**-7).astype(BF)
    mutual_q = jnp.where(hit, 1.0, packed[:, 384:512] * scaling).astype(BF)
    mutual_k = jnp.where(hit, -1e5, packed[:, 512:640]).astype(BF)
    mutual_v = (packed[:, 640:768] * 2.0**-7).astype(BF)
    one = lax.broadcasted_iota(jnp.int32, (128, LANES), 1)
    own = [(one >= h * HEAD) & (one < (h + 1) * HEAD) for h in range(HEADS)]
    own_spare = [m | (one >= C) for m in own]
    self_out, mutual_out = [], []
    for w in range(tokens // 128):
        a = slice(w * 128, (w + 1) * 128)
        self_out.append(attend(self_q[a], self_k[a], self_v[a], own, own, ones))
        mutual_out.append(attend(mutual_q[a], mutual_k[a], mutual_v[a], own_spare, own, ones))
    attended = jnp.concatenate(
        [jnp.concatenate(self_out, 0), jnp.concatenate(mutual_out, 0)], 1
    ).astype(BF)
    middle = (x + dot(attended, proj_w)).astype(BF).astype(F32)
    widened = dot(norm_tokens(middle), in_w)
    gated = (gelu(widened[:, :256]) * widened[:, 256:]).astype(BF)
    return (middle + dot(gated, out_w)).astype(BF)


def pad(w, rows, lanes):
    if lanes > w.shape[1]:
        w = jnp.concatenate([w, jnp.zeros((w.shape[0], lanes - w.shape[1]), w.dtype)], 1)
    if rows > w.shape[0]:
        w = jnp.concatenate([w, jnp.zeros((rows - w.shape[0], lanes), w.dtype)], 0)
    return w


def prepare_weights(l, qkv_ref, proj_ref, in_ref, out_ref, qkv_s, proj_s, in_s, out_s):
    w = qkv_ref[l].astype(F32)
    for i in range(6):
        part = pad(w[:, i * C : (i + 1) * C], LANES, LANES)
        qkv_s[l, :, i * LANES : (i + 1) * LANES] = part.astype(BF)
    w = proj_ref[l].astype(F32)
    for i in range(2):
        proj_s[l, i * LANES : (i + 1) * LANES, :] = pad(w[i * C : (i + 1) * C], LANES, LANES).astype(BF)
    w = in_ref[l].astype(F32)
    for i in range(2):
        in_s[l, :, i * 256 : (i + 1) * 256] = pad(w[:, i * HID : (i + 1) * HID], LANES, 256).astype(BF)
    out_s[l] = pad(out_ref[l].astype(F32), 256, LANES).astype(BF)


def kernel(
    frames_n, tiles_n,
    x_ref, qkv_ref, proj_ref, in_ref, out_ref, o_ref,
    qkv_s, proj_s, in_s, out_s, ones_s, cells, own, halo_t, halo_f, halo_d,
    back, final, send_a, recv_a, send_b, recv_b,
):
    f_me, t_me = lax.axis_index("frame"), lax.axis_index("tile")
    f_up, f_down = lax.rem(f_me + 1, frames_n), lax.rem(f_me + frames_n - 1, frames_n)
    t_up, t_down = lax.rem(t_me + 1, tiles_n), lax.rem(t_me + tiles_n - 1, tiles_n)
    up = ((f_me, t_up), (f_up, t_me), (f_up, t_up))
    down = ((f_me, t_down), (f_down, t_me), (f_down, t_down))
    barrier = pltpu.get_barrier_semaphore()
    for where in up + down:
        pl.semaphore_signal(barrier, inc=1, device_id=where, device_id_type=MESH)

    low = lax.broadcasted_iota(jnp.int32, (4, 8, LANES), 1) < 4
    for f in range(4):
        rows = x_ref[f].astype(F32)
        rows = jnp.concatenate([rows, jnp.zeros((8, 32, LANES - C), F32)], 2).reshape(8, 4, 8, LANES)
        for p in range(4):
            a, b = rows[2 * p], rows[2 * p + 1]
            at = slice(8 * (p % 2), 8 * (p % 2) + 8)
            cells[f, p // 2, 0, :, at, :] = jnp.where(low, a, pltpu.roll(b, 4, 1))
            cells[f, p // 2, 1, :, at, :] = jnp.where(low, pltpu.roll(a, 4, 1), b)

    head = lax.broadcasted_iota(jnp.int32, (128, LANES), 1)
    for h in range(HEADS):
        inside = ((head >= h * HEAD) & (head < (h + 1) * HEAD)) | (head >= C)
        ones_s[h * 128 : (h + 1) * 128, :] = jnp.where(inside, 2.0**-3, 0.0).astype(BF)
    for l in range(2):
        prepare_weights(l, qkv_ref, proj_ref, in_ref, out_ref, qkv_s, proj_s, in_s, out_s)

    def run(x, l):
        return layer(x, qkv_s[l], proj_s[l], in_s[l], out_s[l], ones_s[...])

    def copies_a(n, lo, hi):
        pairs = (
            (own.at[1:4, 0, :, lo:hi], halo_t.at[:, :, lo:hi]),
            (own.at[0, 1, :, lo:hi], halo_f.at[:, lo:hi]),
            (own.at[0, 0, :, lo:hi], halo_d.at[:, lo:hi]),
        )
        return [
            pltpu.make_async_remote_copy(
                src_ref=s, dst_ref=d, send_sem=send_a.at[n, i], recv_sem=recv_a.at[n, i],
                device_id=down[i], device_id_type=MESH,
            )
            for i, (s, d) in enumerate(pairs)
        ]

    def copies_b(n, lo, hi):
        pairs = (
            (back.at[0:3, 1, :, lo:hi], final.at[1:4, 0, :, lo:hi]),
            (back.at[3, 0, :, lo:hi], final.at[0, 1, :, lo:hi]),
            (back.at[3, 1, :, lo:hi], final.at[0, 0, :, lo:hi]),
        )
        return [
            pltpu.make_async_remote_copy(
                src_ref=s, dst_ref=d, send_sem=send_b.at[n, i], recv_sem=recv_b.at[n, i],
                device_id=up[i], device_id_type=MESH,
            )
            for i, (s, d) in enumerate(pairs)
        ]

    first = []
    for n, (lo, hi) in enumerate(FIRST_GROUPS):
        order = [
            (f, q, g, s)
            for s in range(lo, hi) for m in range(2)
            for f in (2 * m, 2 * m + 1) for q in range(2) for g in range(2)
        ]
        y = run(jnp.concatenate([cells[i] for i in order], 0), 0)
        for j, i in enumerate(order):
            own[i] = y[16 * j : 16 * j + 16]
        if n == 0:
            pl.semaphore_wait(barrier, 6)
        first.append(copies_a(n, lo, hi))
        for c in first[-1]:
            c.start()

    def second_cell(f, q, g, s):
        if f < 3:
            return own[f + 1, 1, g, s] if q == 0 else halo_t[f, g, s]
        return halo_f[g, s] if q == 0 else halo_d[g, s]

    arrived = 0
    second = []
    for n, (lo, hi) in enumerate(SECOND_GROUPS):
        need = 4 if hi == 4 else hi + 1
        while arrived < len(FIRST_GROUPS) and FIRST_GROUPS[arrived][0] < need:
            for c in first[arrived]:
                c.wait_recv()
            arrived += 1
        order = [
            (f, q, j, s)
            for s in range(lo, hi) for m in range(2)
            for f in (2 * m, 2 * m + 1) for q in range(2) for j in range(2)
        ]
        x = jnp.concatenate([second_cell(f, q, 1 - j, (s + j) % 4) for f, q, j, s in order], 0)
        y = run(x.astype(F32), 1)
        for i, (f, q, j, s) in enumerate(order):
            part = y[16 * i : 16 * i + 16]
            if f < 3 and q == 0:
                final[f + 1, 1, j, s] = part
            else:
                back[f, q, j, s] = part
        second.append(copies_b(n, lo, hi))
        for c in second[-1]:
            c.start()
    for group in second:
        for c in group:
            c.wait_recv()

    for f in range(4):
        for q in range(2):
            right = final[f, q, 0].astype(F32)
            left = jnp.concatenate([final[f, q, 1, 3:4], final[f, q, 1, 0:3]], 0).astype(F32)
            for h in range(2):
                a, b = left[:, 8 * h : 8 * h + 8], right[:, 8 * h : 8 * h + 8]
                r = 4 * q + 2 * h
                even = jnp.where(low, a, pltpu.roll(b, 4, 1)).reshape(32, LANES)
                odd = jnp.where(low, pltpu.roll(a, 4, 1), b).reshape(32, LANES)
                o_ref[f, r] = even[:, :C].astype(BF)
                o_ref[f, r + 1] = odd[:, :C].astype(BF)
    for group in first + second:
        for c in group:
            c.wait_send()


def local(frames_n, tiles_n, feats, qkv_weight, proj_weight, mlp_in, mlp_out):
    vmem = pl.BlockSpec(memory_space=pltpu.VMEM)
    halo = (2, 4, 16, LANES)
    return pl.pallas_call(
        functools.partial(kernel, frames_n, tiles_n),
        out_shape=jax.ShapeDtypeStruct(feats.shape, feats.dtype),
        in_specs=[vmem] * 5,
        out_specs=vmem,
        scratch_shapes=[
            pltpu.VMEM((2, 128, 768), BF),
            pltpu.VMEM((2, 256, 128), BF),
            pltpu.VMEM((2, 128, 512), BF),
            pltpu.VMEM((2, 256, 128), BF),
            pltpu.VMEM((768, 128), BF),
            pltpu.VMEM((4, 2) + halo, F32),
            pltpu.VMEM((4, 2) + halo, BF),
            pltpu.VMEM((3,) + halo, BF),
            pltpu.VMEM(halo, BF),
            pltpu.VMEM(halo, BF),
            pltpu.VMEM((4, 2) + halo, BF),
            pltpu.VMEM((4, 2) + halo, BF),
            pltpu.SemaphoreType.DMA((len(FIRST_GROUPS), 3)),
            pltpu.SemaphoreType.DMA((len(FIRST_GROUPS), 3)),
            pltpu.SemaphoreType.DMA((len(SECOND_GROUPS), 3)),
            pltpu.SemaphoreType.DMA((len(SECOND_GROUPS), 3)),
        ],
        compiler_params=pltpu.CompilerParams(
            collective_id=0, has_side_effects=True, vmem_limit_bytes=60 << 20
        ),
    )(feats, qkv_weight, proj_weight, mlp_in, mlp_out)


def solution(mesh):
    placed = (P("frame", "tile", None, None), P(), P(), P(), P())
    return jax.shard_map(
        functools.partial(local, mesh.shape["frame"], mesh.shape["tile"]),
        mesh=mesh, in_specs=placed, out_specs=P("frame", "tile", None, None), check_vma=False,
    )
```

```python
import functools

import jax
import jax.numpy as jnp
from jax import lax
from jax.experimental import pallas as pl
from jax.experimental.pallas import tpu as pltpu
from jax.sharding import PartitionSpec as P

C, HEADS, HEAD, HID = 120, 6, 20, 240
LANES = 128
EPSILON = 1e-05
LOG2E = 1.4426950408889634
MESH = pl.DeviceIdType.MESH
FIRST_GROUPS = ((0, 4),)
SECOND_GROUPS = ((0, 4),)
BF, F32 = jnp.bfloat16, jnp.float32


def dot(a, b, dims=(((1,), (0,)), ((), ()))):
    return lax.dot_general(a, b, dims, preferred_element_type=F32)


def norm_tokens(x):
    mean = jnp.sum(x, -1, keepdims=True) * (1.0 / C)
    lane = lax.broadcasted_iota(jnp.int32, x.shape, 1)
    center = jnp.where(lane < C, x - mean, 0.0)
    spread = jnp.sum(center * center, -1, keepdims=True) * (1.0 / C)
    return (center * lax.rsqrt(spread + EPSILON)).astype(BF)


def gelu(g):
    return g * 0.5 * (1.0 + lax.erf(g * 0.7071067811865476))


def attend(q, k, v, key_masks, value_masks, ones):
    kb = jnp.concatenate([jnp.where(m, k, jnp.zeros_like(k)) for m in key_masks], 0)
    weights = jnp.exp2(dot(q, kb, (((1,), (1,)), ((), ())))).astype(BF)
    vb = jnp.concatenate([jnp.where(m, v, jnp.zeros_like(v)) for m in value_masks], 0)
    both = dot(weights, jnp.concatenate([vb, ones], 1))
    return both[:, :LANES] * (pl.reciprocal(both[:, LANES:], approx=False) * 16.0)


def layer(x, qkv_w, proj_w, in_w, out_w, ones):
    tokens = x.shape[0]
    packed = dot(norm_tokens(x), qkv_w)
    scaling = HEAD**-0.5 * LOG2E
    lane = lax.broadcasted_iota(jnp.int32, (tokens, LANES), 1)
    row = lax.broadcasted_iota(jnp.int32, (tokens, LANES), 0)
    hit = lane == C + lax.rem(row // 64, 2)
    self_q = (packed[:, 0:128] * scaling).astype(BF)
    self_k = packed[:, 128:256].astype(BF)
    self_v = (packed[:, 256:384] * 2.0**-7).astype(BF)
    mutual_q = jnp.where(hit, 1.0, packed[:, 384:512] * scaling).astype(BF)
    mutual_k = jnp.where(hit, -1e5, packed[:, 512:640]).astype(BF)
    mutual_v = (packed[:, 640:768] * 2.0**-7).astype(BF)
    one = lax.broadcasted_iota(jnp.int32, (128, LANES), 1)
    own = [(one >= h * HEAD) & (one < (h + 1) * HEAD) for h in range(HEADS)]
    own_spare = [m | (one >= C) for m in own]
    self_out, mutual_out = [], []
    for w in range(tokens // 128):
        a = slice(w * 128, (w + 1) * 128)
        self_out.append(attend(self_q[a], self_k[a], self_v[a], own, own, ones))
        mutual_out.append(attend(mutual_q[a], mutual_k[a], mutual_v[a], own_spare, own, ones))
    attended = jnp.concatenate(
        [jnp.concatenate(self_out, 0), jnp.concatenate(mutual_out, 0)], 1
    ).astype(BF)
    middle = (x + dot(attended, proj_w)).astype(BF).astype(F32)
    widened = dot(norm_tokens(middle), in_w)
    gated = (gelu(widened[:, :256]) * widened[:, 256:]).astype(BF)
    return (middle + dot(gated, out_w)).astype(BF)


def pad(w, rows, lanes):
    if lanes > w.shape[1]:
        w = jnp.concatenate([w, jnp.zeros((w.shape[0], lanes - w.shape[1]), w.dtype)], 1)
    if rows > w.shape[0]:
        w = jnp.concatenate([w, jnp.zeros((rows - w.shape[0], lanes), w.dtype)], 0)
    return w


def prepare_weights(l, qkv_ref, proj_ref, in_ref, out_ref, qkv_s, proj_s, in_s, out_s):
    w = qkv_ref[l].astype(F32)
    for i in range(6):
        part = pad(w[:, i * C : (i + 1) * C], LANES, LANES)
        qkv_s[l, :, i * LANES : (i + 1) * LANES] = part.astype(BF)
    w = proj_ref[l].astype(F32)
    for i in range(2):
        proj_s[l, i * LANES : (i + 1) * LANES, :] = pad(w[i * C : (i + 1) * C], LANES, LANES).astype(BF)
    w = in_ref[l].astype(F32)
    for i in range(2):
        in_s[l, :, i * 256 : (i + 1) * 256] = pad(w[:, i * HID : (i + 1) * HID], LANES, 256).astype(BF)
    out_s[l] = pad(out_ref[l].astype(F32), 256, LANES).astype(BF)


def kernel(
    frames_n, tiles_n,
    x_ref, qkv_ref, proj_ref, in_ref, out_ref, o_ref,
    qkv_s, proj_s, in_s, out_s, ones_s, cells, own, halo_t, halo_f, halo_d,
    back, final, send_a, recv_a, send_b, recv_b,
):
    f_me, t_me = lax.axis_index("frame"), lax.axis_index("tile")
    f_up, f_down = lax.rem(f_me + 1, frames_n), lax.rem(f_me + frames_n - 1, frames_n)
    t_up, t_down = lax.rem(t_me + 1, tiles_n), lax.rem(t_me + tiles_n - 1, tiles_n)
    up = ((f_me, t_up), (f_up, t_me), (f_up, t_up))
    down = ((f_me, t_down), (f_down, t_me), (f_down, t_down))
    barrier = pltpu.get_barrier_semaphore()
    for where in up + down:
        pl.semaphore_signal(barrier, inc=1, device_id=where, device_id_type=MESH)

    low = lax.broadcasted_iota(jnp.int32, (4, 8, LANES), 1) < 4
    for f in range(4):
        rows = x_ref[f].astype(F32)
        rows = jnp.concatenate([rows, jnp.zeros((8, 32, LANES - C), F32)], 2).reshape(8, 4, 8, LANES)
        for p in range(4):
            a, b = rows[2 * p], rows[2 * p + 1]
            at = slice(8 * (p % 2), 8 * (p % 2) + 8)
            cells[f, p // 2, 0, :, at, :] = jnp.where(low, a, pltpu.roll(b, 4, 1))
            cells[f, p // 2, 1, :, at, :] = jnp.where(low, pltpu.roll(a, 4, 1), b)

    head = lax.broadcasted_iota(jnp.int32, (128, LANES), 1)
    for h in range(HEADS):
        inside = ((head >= h * HEAD) & (head < (h + 1) * HEAD)) | (head >= C)
        ones_s[h * 128 : (h + 1) * 128, :] = jnp.where(inside, 2.0**-3, 0.0).astype(BF)
    for l in range(2):
        prepare_weights(l, qkv_ref, proj_ref, in_ref, out_ref, qkv_s, proj_s, in_s, out_s)

    def run(x, l):
        return layer(x, qkv_s[l], proj_s[l], in_s[l], out_s[l], ones_s[...])

    def copies_a(n, lo, hi):
        pairs = (
            (own.at[0:3, 1, :, lo:hi], halo_t.at[:, :, lo:hi]),
            (own.at[3, 0, :, lo:hi], halo_f.at[:, lo:hi]),
            (own.at[3, 1, :, lo:hi], halo_d.at[:, lo:hi]),
        )
        return [
            pltpu.make_async_remote_copy(
                src_ref=s, dst_ref=d, send_sem=send_a.at[n, i], recv_sem=recv_a.at[n, i],
                device_id=up[i], device_id_type=MESH,
            )
            for i, (s, d) in enumerate(pairs)
        ]

    def copies_b(n, lo, hi):
        pairs = (
            (back.at[1:4, 0, :, lo:hi], final.at[0:3, 1, :, lo:hi]),
            (back.at[0, 1, :, lo:hi], final.at[3, 0, :, lo:hi]),
            (back.at[0, 0, :, lo:hi], final.at[3, 1, :, lo:hi]),
        )
        return [
            pltpu.make_async_remote_copy(
                src_ref=s, dst_ref=d, send_sem=send_b.at[n, i], recv_sem=recv_b.at[n, i],
                device_id=down[i], device_id_type=MESH,
            )
            for i, (s, d) in enumerate(pairs)
        ]

    first = []
    for n, (lo, hi) in enumerate(FIRST_GROUPS):
        order = [
            (f, q, g, s)
            for s in range(lo, hi) for m in range(2)
            for f in (2 * m, 2 * m + 1) for q in range(2) for g in range(2)
        ]
        y = run(jnp.concatenate([cells[i] for i in order], 0), 0)
        for j, i in enumerate(order):
            own[i] = y[16 * j : 16 * j + 16]
        if n == 0:
            pl.semaphore_wait(barrier, 6)
        first.append(copies_a(n, lo, hi))
        for c in first[-1]:
            c.start()

    def second_cell(f, q, g, s):
        if f > 0:
            return own[f - 1, 0, g, s] if q == 1 else halo_t[f - 1, g, s]
        return halo_f[g, s] if q == 1 else halo_d[g, s]

    arrived = 0
    second = []
    for n, (lo, hi) in enumerate(SECOND_GROUPS):
        need = 4 if hi == 4 else hi + 1
        while arrived < len(FIRST_GROUPS) and FIRST_GROUPS[arrived][0] < need:
            for c in first[arrived]:
                c.wait_recv()
            arrived += 1
        order = [
            (f, q, j, s)
            for s in range(lo, hi) for m in range(2)
            for f in (2 * m, 2 * m + 1) for q in range(2) for j in range(2)
        ]
        x = jnp.concatenate([second_cell(f, q, 1 - j, (s + j) % 4) for f, q, j, s in order], 0)
        y = run(x.astype(F32), 1)
        for i, (f, q, j, s) in enumerate(order):
            part = y[16 * i : 16 * i + 16]
            if f > 0 and q == 1:
                final[f - 1, 0, j, s] = part
            else:
                back[f, q, j, s] = part
        second.append(copies_b(n, lo, hi))
        for c in second[-1]:
            c.start()
    for group in second:
        for c in group:
            c.wait_recv()

    for f in range(4):
        for q in range(2):
            right = final[f, q, 0].astype(F32)
            left = jnp.concatenate([final[f, q, 1, 3:4], final[f, q, 1, 0:3]], 0).astype(F32)
            for h in range(2):
                a, b = left[:, 8 * h : 8 * h + 8], right[:, 8 * h : 8 * h + 8]
                r = 4 * q + 2 * h
                even = jnp.where(low, a, pltpu.roll(b, 4, 1)).reshape(32, LANES)
                odd = jnp.where(low, pltpu.roll(a, 4, 1), b).reshape(32, LANES)
                o_ref[f, r] = even[:, :C].astype(BF)
                o_ref[f, r + 1] = odd[:, :C].astype(BF)
    for group in first + second:
        for c in group:
            c.wait_send()


def local(frames_n, tiles_n, feats, qkv_weight, proj_weight, mlp_in, mlp_out):
    vmem = pl.BlockSpec(memory_space=pltpu.VMEM)
    halo = (2, 4, 16, LANES)
    return pl.pallas_call(
        functools.partial(kernel, frames_n, tiles_n),
        out_shape=jax.ShapeDtypeStruct(feats.shape, feats.dtype),
        in_specs=[vmem] * 5,
        out_specs=vmem,
        scratch_shapes=[
            pltpu.VMEM((2, 128, 768), BF),
            pltpu.VMEM((2, 256, 128), BF),
            pltpu.VMEM((2, 128, 512), BF),
            pltpu.VMEM((2, 256, 128), BF),
            pltpu.VMEM((768, 128), BF),
            pltpu.VMEM((4, 2) + halo, F32),
            pltpu.VMEM((4, 2) + halo, BF),
            pltpu.VMEM((3,) + halo, BF),
            pltpu.VMEM(halo, BF),
            pltpu.VMEM(halo, BF),
            pltpu.VMEM((4, 2) + halo, BF),
            pltpu.VMEM((4, 2) + halo, BF),
            pltpu.SemaphoreType.DMA((len(FIRST_GROUPS), 3)),
            pltpu.SemaphoreType.DMA((len(FIRST_GROUPS), 3)),
            pltpu.SemaphoreType.DMA((len(SECOND_GROUPS), 3)),
            pltpu.SemaphoreType.DMA((len(SECOND_GROUPS), 3)),
        ],
        compiler_params=pltpu.CompilerParams(
            collective_id=0, has_side_effects=True, vmem_limit_bytes=60 << 20
        ),
    )(feats, qkv_weight, proj_weight, mlp_in, mlp_out)


def solution(mesh):
    placed = (P("frame", "tile", None, None), P(), P(), P(), P())
    return jax.shard_map(
        functools.partial(local, mesh.shape["frame"], mesh.shape["tile"]),
        mesh=mesh, in_specs=placed, out_specs=P("frame", "tile", None, None), check_vma=False,
    )
```

```python
import functools

import jax
import jax.numpy as jnp
from jax import lax
from jax.experimental import pallas as pl
from jax.experimental.pallas import tpu as pltpu
from jax.sharding import PartitionSpec as P

C, HEADS, HEAD, HID = 120, 6, 20, 240
LANES = 128
EPSILON = 1e-05
LOG2E = 1.4426950408889634
MESH = pl.DeviceIdType.MESH
FIRST_GROUPS = ((0, 4),)
BF, F32 = jnp.bfloat16, jnp.float32


def dot(a, b, dims=(((1,), (0,)), ((), ()))):
    return lax.dot_general(a, b, dims, preferred_element_type=F32)


def norm_tokens(x):
    mean = jnp.sum(x, -1, keepdims=True) * (1.0 / C)
    lane = lax.broadcasted_iota(jnp.int32, x.shape, 1)
    center = jnp.where(lane < C, x - mean, 0.0)
    spread = jnp.sum(center * center, -1, keepdims=True) * (1.0 / C)
    return (center * lax.rsqrt(spread + EPSILON)).astype(BF)


def gelu(g):
    return g * 0.5 * (1.0 + lax.erf(g * 0.7071067811865476))


def attend(q, k, v, key_masks, value_masks, ones):
    kb = jnp.concatenate([jnp.where(m, k, jnp.zeros_like(k)) for m in key_masks], 0)
    weights = jnp.exp2(dot(q, kb, (((1,), (1,)), ((), ())))).astype(BF)
    vb = jnp.concatenate([jnp.where(m, v, jnp.zeros_like(v)) for m in value_masks], 0)
    both = dot(weights, jnp.concatenate([vb, ones], 1))
    return both[:, :LANES] * (pl.reciprocal(both[:, LANES:], approx=False) * 16.0)


def layer(x, qkv_w, proj_w, in_w, out_w, ones):
    tokens = x.shape[0]
    packed = dot(norm_tokens(x), qkv_w)
    scaling = HEAD**-0.5 * LOG2E
    lane = lax.broadcasted_iota(jnp.int32, (tokens, LANES), 1)
    row = lax.broadcasted_iota(jnp.int32, (tokens, LANES), 0)
    hit = lane == C + lax.rem(row // 64, 2)
    self_q = (packed[:, 0:128] * scaling).astype(BF)
    self_k = packed[:, 128:256].astype(BF)
    self_v = (packed[:, 256:384] * 2.0**-7).astype(BF)
    mutual_q = jnp.where(hit, 1.0, packed[:, 384:512] * scaling).astype(BF)
    mutual_k = jnp.where(hit, -1e5, packed[:, 512:640]).astype(BF)
    mutual_v = (packed[:, 640:768] * 2.0**-7).astype(BF)
    one = lax.broadcasted_iota(jnp.int32, (128, LANES), 1)
    own = [(one >= h * HEAD) & (one < (h + 1) * HEAD) for h in range(HEADS)]
    own_spare = [m | (one >= C) for m in own]
    self_out, mutual_out = [], []
    for w in range(tokens // 128):
        a = slice(w * 128, (w + 1) * 128)
        self_out.append(attend(self_q[a], self_k[a], self_v[a], own, own, ones))
        mutual_out.append(attend(mutual_q[a], mutual_k[a], mutual_v[a], own_spare, own, ones))
    attended = jnp.concatenate(
        [jnp.concatenate(self_out, 0), jnp.concatenate(mutual_out, 0)], 1
    ).astype(BF)
    return finish(x, attended, proj_w, in_w, out_w)


def finish(x, attended, proj_w, in_w, out_w):
    middle = (x + dot(attended, proj_w)).astype(BF).astype(F32)
    widened = dot(norm_tokens(middle), in_w)
    gated = (gelu(widened[:, :256]) * widened[:, 256:]).astype(BF)
    return (middle + dot(gated, out_w)).astype(BF)


def attend_rows(q_self, q_mutual, k_self, k_mutual, v_self, v_mutual):
    n = q_self.shape[0]
    one = lax.broadcasted_iota(jnp.int32, (n, LANES), 1)
    own = [(one >= h * HEAD) & (one < (h + 1) * HEAD) for h in range(HEADS)]
    none, zero = jnp.zeros_like(q_self), jnp.zeros_like(k_self)

    def sides(a, b):
        return jnp.concatenate([jnp.concatenate([a, zero], 1), jnp.concatenate([zero, b], 1)], 0)

    stack = jnp.concatenate(
        [
            jnp.concatenate(
                [jnp.where(m, q_self, none), jnp.where(m | (one >= C), q_mutual, none)], 1
            )
            for m in own
        ],
        0,
    )
    scores = dot(stack, sides(k_self, k_mutual), (((1,), (1,)), ((), ())))
    both = dot(jnp.exp2(scores).astype(BF), sides(v_self, v_mutual))
    out = jnp.zeros((n, 2 * LANES), F32)
    for h, m in enumerate(own):
        keep = m | (one == C + h)
        keep = jnp.concatenate([keep, keep], 1)
        out = jnp.where(keep, both[h * n : (h + 1) * n], out)
    return out


def second_layer_side(x, own_normed, all_normed, q_w, kv_w, proj_w, in_w, out_w, spread):
    scaling = HEAD**-0.5 * LOG2E
    query = dot(own_normed, q_w) * scaling
    lane = lax.broadcasted_iota(jnp.int32, (query.shape[0], LANES), 1)
    row = lax.broadcasted_iota(jnp.int32, (query.shape[0], LANES), 0)
    hit = lane == C + 1 - lax.rem(row // 32, 2)
    self_q = query[:, :LANES].astype(BF)
    mutual_q = jnp.where(hit, 1.0, query[:, LANES:]).astype(BF)
    packed = dot(all_normed, kv_w)
    lane = lax.broadcasted_iota(jnp.int32, (packed.shape[0], LANES), 1)
    row = lax.broadcasted_iota(jnp.int32, (packed.shape[0], LANES), 0)
    hit = lane == C + lax.rem(row // 64, 2)
    self_k = packed[:, 0:128].astype(BF)
    mutual_k = jnp.where(hit, -1e5, packed[:, 128:256]).astype(BF)
    self_v = jnp.where(lane >= C, 2.0**-3, packed[:, 256:384] * 2.0**-7).astype(BF)
    mutual_v = jnp.where(lane >= C, 2.0**-3, packed[:, 384:512] * 2.0**-7).astype(BF)
    sums = []
    for s in range(query.shape[0] // 128):
        for first, last, pair in ((0, 32, 0), (32, 96, 1), (96, 128, 2)):
            a = slice(128 * s + first, 128 * s + last)
            b = slice(384 * s + 128 * pair, 384 * s + 128 * pair + 128)
            sums.append(
                attend_rows(self_q[a], mutual_q[a], self_k[b], mutual_k[b], self_v[b], mutual_v[b])
            )
    sums = jnp.concatenate(sums, 0)
    lane = lax.rem(lax.broadcasted_iota(jnp.int32, sums.shape, 1), LANES)
    held = (lane >= C) & (lane < C + HEADS)
    inverse = jnp.where(held, pl.reciprocal(jnp.where(held, sums, 1.0), approx=False) * 16.0, 0.0)
    high = inverse.astype(BF)
    low = (inverse - high.astype(F32)).astype(BF)
    attended = (sums * (dot(high, spread) + dot(low, spread))).astype(BF)
    return finish(x, attended, proj_w, in_w, out_w)


def pad(w, rows, lanes):
    if lanes > w.shape[1]:
        w = jnp.concatenate([w, jnp.zeros((w.shape[0], lanes - w.shape[1]), w.dtype)], 1)
    if rows > w.shape[0]:
        w = jnp.concatenate([w, jnp.zeros((rows - w.shape[0], lanes), w.dtype)], 0)
    return w


def prepare_weights(l, qkv_ref, proj_ref, in_ref, out_ref, qkv_s, proj_s, in_s, out_s):
    w = qkv_ref[l].astype(F32)
    for i in range(6):
        part = pad(w[:, i * C : (i + 1) * C], LANES, LANES)
        at = i if l == 0 else (0, 2, 4, 1, 3, 5)[i]
        qkv_s[l, :, at * LANES : (at + 1) * LANES] = part.astype(BF)
    w = proj_ref[l].astype(F32)
    for i in range(2):
        proj_s[l, i * LANES : (i + 1) * LANES, :] = pad(w[i * C : (i + 1) * C], LANES, LANES).astype(BF)
    w = in_ref[l].astype(F32)
    for i in range(2):
        in_s[l, :, i * 256 : (i + 1) * 256] = pad(w[:, i * HID : (i + 1) * HID], LANES, 256).astype(BF)
    out_s[l] = pad(out_ref[l].astype(F32), 256, LANES).astype(BF)


def kernel(
    frames_n, tiles_n,
    x_ref, qkv_ref, proj_ref, in_ref, out_ref, o_ref,
    qkv_s, proj_s, in_s, out_s, ones_s, spread_s, cells, own, normed, next_t, last_t, last_f, next_f,
    final, send, recv,
):
    f_me, t_me = lax.axis_index("frame"), lax.axis_index("tile")
    f_up, f_down = lax.rem(f_me + 1, frames_n), lax.rem(f_me + frames_n - 1, frames_n)
    t_up, t_down = lax.rem(t_me + 1, tiles_n), lax.rem(t_me + tiles_n - 1, tiles_n)
    targets = (
        (f_me, t_down), (f_up, t_down), (f_down, t_down), (f_up, t_me), (f_down, t_me),
        (f_me, t_up), (f_up, t_up), (f_down, t_up),
    )
    barrier = pltpu.get_barrier_semaphore()
    for where in targets:
        pl.semaphore_signal(barrier, inc=1, device_id=where, device_id_type=MESH)

    low = lax.broadcasted_iota(jnp.int32, (4, 8, LANES), 1) < 4
    for f in range(4):
        rows = x_ref[f].astype(F32)
        rows = jnp.concatenate([rows, jnp.zeros((8, 32, LANES - C), F32)], 2).reshape(8, 4, 8, LANES)
        for p in range(4):
            a, b = rows[2 * p], rows[2 * p + 1]
            at = slice(8 * (p % 2), 8 * (p % 2) + 8)
            cells[f, p // 2, 0, :, at, :] = jnp.where(low, a, pltpu.roll(b, 4, 1))
            cells[f, p // 2, 1, :, at, :] = jnp.where(low, pltpu.roll(a, 4, 1), b)

    head = lax.broadcasted_iota(jnp.int32, (128, LANES), 1)
    for h in range(HEADS):
        inside = ((head >= h * HEAD) & (head < (h + 1) * HEAD)) | (head >= C)
        ones_s[h * 128 : (h + 1) * 128, :] = jnp.where(inside, 2.0**-3, 0.0).astype(BF)
    r = lax.broadcasted_iota(jnp.int32, (256, 256), 0)
    c = lax.broadcasted_iota(jnp.int32, (256, 256), 1)
    start = (lax.rem(r, LANES) - C) * HEAD
    column = lax.rem(c, LANES)
    hits = (lax.rem(r, LANES) >= C) & (column >= start) & (column < start + HEAD) & (column < C)
    hits = hits & (r // LANES == c // LANES)
    spread_s[...] = jnp.where(hits, 1.0, 0.0).astype(BF)
    for l in range(2):
        prepare_weights(l, qkv_ref, proj_ref, in_ref, out_ref, qkv_s, proj_s, in_s, out_s)

    def copies(n, lo, hi):
        pairs = (
            (normed.at[:, 0, :, lo:hi], next_t.at[1:5, :, lo:hi]),
            (normed.at[3, 0, :, lo:hi], next_t.at[0, :, lo:hi]),
            (normed.at[0, 0, :, lo:hi], next_t.at[5, :, lo:hi]),
            (normed.at[3, :, :, lo:hi], last_f.at[:, :, lo:hi]),
            (normed.at[0, :, :, lo:hi], next_f.at[:, :, lo:hi]),
            (normed.at[:, 1, :, lo:hi], last_t.at[1:5, :, lo:hi]),
            (normed.at[3, 1, :, lo:hi], last_t.at[0, :, lo:hi]),
            (normed.at[0, 1, :, lo:hi], last_t.at[5, :, lo:hi]),
        )
        return [
            pltpu.make_async_remote_copy(
                src_ref=s, dst_ref=d, send_sem=send.at[n, i], recv_sem=recv.at[n, i],
                device_id=targets[i], device_id_type=MESH,
            )
            for i, (s, d) in enumerate(pairs)
        ]

    sent = []
    for n, (lo, hi) in enumerate(FIRST_GROUPS):
        order = [
            (f, q, g, s)
            for s in range(lo, hi) for m in range(2)
            for f in (2 * m, 2 * m + 1) for q in range(2) for g in range(2)
        ]
        x = jnp.concatenate([cells[i] for i in order], 0)
        y = layer(x, qkv_s[0], proj_s[0], in_s[0], out_s[0], ones_s[...])
        z = norm_tokens(y.astype(F32))
        for j, i in enumerate(order):
            own[i] = y[16 * j : 16 * j + 16]
            normed[i] = z[16 * j : 16 * j + 16]
        if n == 0:
            pl.semaphore_wait(barrier, 8)
        sent.append(copies(n, lo, hi))
        for c in sent[-1]:
            c.start()

    def write_out(q):
        for f in range(4):
            right = final[f, q, 0].astype(F32)
            left = jnp.concatenate([final[f, q, 1, 3:4], final[f, q, 1, 0:3]], 0).astype(F32)
            for h in range(2):
                a, b = left[:, 8 * h : 8 * h + 8], right[:, 8 * h : 8 * h + 8]
                r = 4 * q + 2 * h
                even = jnp.where(low, a, pltpu.roll(b, 4, 1)).reshape(32, LANES)
                odd = jnp.where(low, pltpu.roll(a, 4, 1), b).reshape(32, LANES)
                o_ref[f, r] = even[:, :C].astype(BF)
                o_ref[f, r + 1] = odd[:, :C].astype(BF)

    def side(q, halo, arrivals):
        for group in sent:
            for i in arrivals:
                group[i].wait_recv()

        def beside(f, g, s):
            if f < 0:
                return last_f[q, g, s]
            return next_f[q, g, s] if f > 3 else normed[f, q, g, s]

        columns = [((1, s), (0, (s + 1) % 4)) for s in range(4)]
        mine = [(f, j, s) for s in range(4) for f in range(4) for j in range(2)]
        x = jnp.concatenate([own[(f, q) + columns[s][j]] for f, j, s in mine], 0).astype(F32)
        own_normed = jnp.concatenate([normed[(f, q) + columns[s][j]] for f, j, s in mine], 0)
        every = []
        for s in range(4):
            for f in range(-1, 5):
                every += [beside(f, *columns[s][j]) for j in range(2)]
                every += [halo[(f + 1,) + columns[s][j]] for j in range(2)]
        y = second_layer_side(
            x, own_normed, jnp.concatenate(every, 0), qkv_s[1, :, 0:256], qkv_s[1, :, 256:768],
            proj_s[1], in_s[1], out_s[1], spread_s[...],
        )
        for i, (f, j, s) in enumerate(mine):
            final[f, q, j, s] = y[16 * i : 16 * i + 16]

    side(1, next_t, (0, 1, 2, 3, 4))
    side(0, last_t, (5, 6, 7))
    write_out(1)
    write_out(0)
    for group in sent:
        for c in group:
            c.wait_send()


def local(frames_n, tiles_n, feats, qkv_weight, proj_weight, mlp_in, mlp_out):
    vmem = pl.BlockSpec(memory_space=pltpu.VMEM)
    halo = (2, 4, 16, LANES)
    return pl.pallas_call(
        functools.partial(kernel, frames_n, tiles_n),
        out_shape=jax.ShapeDtypeStruct(feats.shape, feats.dtype),
        in_specs=[vmem] * 5,
        out_specs=vmem,
        scratch_shapes=[
            pltpu.VMEM((2, 128, 768), BF),
            pltpu.VMEM((2, 256, 128), BF),
            pltpu.VMEM((2, 128, 512), BF),
            pltpu.VMEM((2, 256, 128), BF),
            pltpu.VMEM((768, 128), BF),
            pltpu.VMEM((256, 256), BF),
            pltpu.VMEM((4, 2) + halo, F32),
            pltpu.VMEM((4, 2) + halo, BF),
            pltpu.VMEM((4, 2) + halo, BF),
            pltpu.VMEM((6,) + halo, BF),
            pltpu.VMEM((6,) + halo, BF),
            pltpu.VMEM((2,) + halo, BF),
            pltpu.VMEM((2,) + halo, BF),
            pltpu.VMEM((4, 2) + halo, BF),
            pltpu.SemaphoreType.DMA((len(FIRST_GROUPS), 8)),
            pltpu.SemaphoreType.DMA((len(FIRST_GROUPS), 8)),
        ],
        compiler_params=pltpu.CompilerParams(
            collective_id=0, has_side_effects=True, vmem_limit_bytes=60 << 20
        ),
    )(feats, qkv_weight, proj_weight, mlp_in, mlp_out)


def solution(mesh):
    placed = (P("frame", "tile", None, None), P(), P(), P(), P())
    return jax.shard_map(
        functools.partial(local, mesh.shape["frame"], mesh.shape["tile"]),
        mesh=mesh, in_specs=placed, out_specs=P("frame", "tile", None, None), check_vma=False,
    )
```

```python
import functools

import jax
import jax.numpy as jnp
from jax import lax
from jax.experimental import pallas as pl
from jax.experimental.pallas import tpu as pltpu
from jax.sharding import PartitionSpec as P

C, HEADS, HEAD, HID = 120, 6, 20, 240
LANES = 128
EPSILON = 1e-05
LOG2E = 1.4426950408889634
MESH = pl.DeviceIdType.MESH
FIRST_GROUPS = ((0, 4),)
AHEAD = 2
BF, F32 = jnp.bfloat16, jnp.float32


def dot(a, b, dims=(((1,), (0,)), ((), ()))):
    return lax.dot_general(a, b, dims, preferred_element_type=F32)


def norm_tokens(x):
    mean = jnp.sum(x, -1, keepdims=True) * (1.0 / C)
    lane = lax.broadcasted_iota(jnp.int32, x.shape, 1)
    center = jnp.where(lane < C, x - mean, 0.0)
    spread = jnp.sum(center * center, -1, keepdims=True) * (1.0 / C)
    return (center * lax.rsqrt(spread + EPSILON)).astype(BF)


def gelu(g):
    return g * 0.5 * (1.0 + lax.erf(g * 0.7071067811865476))


def attend(q, k, v, key_masks, value_masks, ones):
    kb = jnp.concatenate([jnp.where(m, k, jnp.zeros_like(k)) for m in key_masks], 0)
    weights = jnp.exp2(dot(q, kb, (((1,), (1,)), ((), ())))).astype(BF)
    vb = jnp.concatenate([jnp.where(m, v, jnp.zeros_like(v)) for m in value_masks], 0)
    both = dot(weights, jnp.concatenate([vb, ones], 1))
    return both[:, :LANES] * (pl.reciprocal(both[:, LANES:], approx=False) * 16.0)


def layer(x, qkv_w, proj_w, in_w, out_w, ones):
    tokens = x.shape[0]
    packed = dot(norm_tokens(x), qkv_w)
    scaling = HEAD**-0.5 * LOG2E
    lane = lax.broadcasted_iota(jnp.int32, (tokens, LANES), 1)
    row = lax.broadcasted_iota(jnp.int32, (tokens, LANES), 0)
    hit = lane == C + lax.rem(row // 64, 2)
    self_q = (packed[:, 0:128] * scaling).astype(BF)
    self_k = packed[:, 128:256].astype(BF)
    self_v = (packed[:, 256:384] * 2.0**-7).astype(BF)
    mutual_q = jnp.where(hit, 1.0, packed[:, 384:512] * scaling).astype(BF)
    mutual_k = jnp.where(hit, -1e5, packed[:, 512:640]).astype(BF)
    mutual_v = (packed[:, 640:768] * 2.0**-7).astype(BF)
    one = lax.broadcasted_iota(jnp.int32, (128, LANES), 1)
    own = [(one >= h * HEAD) & (one < (h + 1) * HEAD) for h in range(HEADS)]
    own_spare = [m | (one >= C) for m in own]
    self_out, mutual_out = [], []
    for w in range(tokens // 128):
        a = slice(w * 128, (w + 1) * 128)
        self_out.append(attend(self_q[a], self_k[a], self_v[a], own, own, ones))
        mutual_out.append(attend(mutual_q[a], mutual_k[a], mutual_v[a], own_spare, own, ones))
    attended = jnp.concatenate(
        [jnp.concatenate(self_out, 0), jnp.concatenate(mutual_out, 0)], 1
    ).astype(BF)
    return finish(x, attended, proj_w, in_w, out_w)


def finish(x, attended, proj_w, in_w, out_w):
    middle = (x + dot(attended, proj_w)).astype(BF).astype(F32)
    widened = dot(norm_tokens(middle), in_w)
    gated = (gelu(widened[:, :256]) * widened[:, 256:]).astype(BF)
    return (middle + dot(gated, out_w)).astype(BF)


def side_by_side(a, b):
    zero = jnp.zeros_like(a)
    return jnp.concatenate([jnp.concatenate([a, zero], 1), jnp.concatenate([zero, b], 1)], 0)


def score_rows(q_self, q_mutual, k_self, k_mutual):
    one = lax.broadcasted_iota(jnp.int32, q_self.shape, 1)
    none = jnp.zeros_like(q_self)
    stack = []
    for h in range(HEADS):
        m = (one >= h * HEAD) & (one < (h + 1) * HEAD)
        parts = [jnp.where(m, q_self, none), jnp.where(m | (one >= C), q_mutual, none)]
        stack.append(jnp.concatenate(parts, 1))
    keys = side_by_side(k_self, k_mutual)
    return dot(jnp.concatenate(stack, 0), keys, (((1,), (1,)), ((), ())))


def weigh_rows(scores, v_self, v_mutual):
    both = dot(jnp.exp2(scores).astype(BF), side_by_side(v_self, v_mutual))
    n = scores.shape[0] // HEADS
    lane = lax.rem(lax.broadcasted_iota(jnp.int32, (n, 2 * LANES), 1), LANES)
    out = jnp.zeros((n, 2 * LANES), F32)
    for h in range(HEADS):
        keep = ((lane >= h * HEAD) & (lane < (h + 1) * HEAD)) | (lane == C + h)
        out = jnp.where(keep, both[h * n : (h + 1) * n], out)
    return out


def second_queries(own_normed, q_w):
    query = dot(own_normed, q_w) * (HEAD**-0.5 * LOG2E)
    lane = lax.broadcasted_iota(jnp.int32, (query.shape[0], LANES), 1)
    row = lax.broadcasted_iota(jnp.int32, (query.shape[0], LANES), 0)
    hit = lane == C + 1 - lax.rem(row // 32, 2)
    return query[:, :LANES].astype(BF), jnp.where(hit, 1.0, query[:, LANES:]).astype(BF)


def second_keys(normed, kv_w):
    packed = dot(normed, kv_w)
    lane = lax.broadcasted_iota(jnp.int32, (packed.shape[0], LANES), 1)
    row = lax.broadcasted_iota(jnp.int32, (packed.shape[0], LANES), 0)
    hit = lane == C + lax.rem(row // 32, 2)
    return (
        packed[:, 0:128].astype(BF),
        jnp.where(hit, -1e5, packed[:, 128:256]).astype(BF),
        jnp.where(lane >= C, 2.0**-3, packed[:, 256:384] * 2.0**-7).astype(BF),
        jnp.where(lane >= C, 2.0**-3, packed[:, 384:512] * 2.0**-7).astype(BF),
    )


def second_layer_side(x, queries, near, far, proj_w, in_w, out_w, spread):
    windows = []
    for s in range(x.shape[0] // 128):
        for first, last, pair in ((0, 32, 0), (32, 96, 1), (96, 128, 2)):
            b = slice(192 * s + 64 * pair, 192 * s + 64 * pair + 64)
            kv = [jnp.concatenate([n[b], f[b]], 0) for n, f in zip(near, far)]
            windows.append([q[128 * s + first : 128 * s + last] for q in queries] + kv)
    scores, sums = [], []
    for w in range(len(windows) + AHEAD):
        if w < len(windows):
            scores.append(score_rows(*windows[w][:4]))
        if w >= AHEAD:
            sums.append(weigh_rows(scores[w - AHEAD], *windows[w - AHEAD][4:]))
    sums = jnp.concatenate(sums, 0)
    lane = lax.rem(lax.broadcasted_iota(jnp.int32, sums.shape, 1), LANES)
    held = (lane >= C) & (lane < C + HEADS)
    inverse = jnp.where(held, pl.reciprocal(jnp.where(held, sums, 1.0), approx=False) * 16.0, 0.0)
    high = inverse.astype(BF)
    low = (inverse - high.astype(F32)).astype(BF)
    attended = (sums * (dot(high, spread) + dot(low, spread))).astype(BF)
    return finish(x, attended, proj_w, in_w, out_w)


def pad(w, rows, lanes):
    if lanes > w.shape[1]:
        w = jnp.concatenate([w, jnp.zeros((w.shape[0], lanes - w.shape[1]), w.dtype)], 1)
    if rows > w.shape[0]:
        w = jnp.concatenate([w, jnp.zeros((rows - w.shape[0], lanes), w.dtype)], 0)
    return w


def prepare_weights(l, qkv_ref, proj_ref, in_ref, out_ref, qkv_s, proj_s, in_s, out_s):
    w = qkv_ref[l].astype(F32)
    for i in range(6):
        part = pad(w[:, i * C : (i + 1) * C], LANES, LANES)
        at = i if l == 0 else (0, 2, 4, 1, 3, 5)[i]
        qkv_s[l, :, at * LANES : (at + 1) * LANES] = part.astype(BF)
    w = proj_ref[l].astype(F32)
    for i in range(2):
        proj_s[l, i * LANES : (i + 1) * LANES, :] = pad(w[i * C : (i + 1) * C], LANES, LANES).astype(BF)
    w = in_ref[l].astype(F32)
    for i in range(2):
        in_s[l, :, i * 256 : (i + 1) * 256] = pad(w[:, i * HID : (i + 1) * HID], LANES, 256).astype(BF)
    out_s[l] = pad(out_ref[l].astype(F32), 256, LANES).astype(BF)


def kernel(
    frames_n, tiles_n,
    x_ref, qkv_ref, proj_ref, in_ref, out_ref, o_ref,
    qkv_s, proj_s, in_s, out_s, ones_s, spread_s, cells, own, normed, next_t, last_t, last_f, next_f,
    send, recv,
):
    f_me, t_me = lax.axis_index("frame"), lax.axis_index("tile")
    f_up, f_down = lax.rem(f_me + 1, frames_n), lax.rem(f_me + frames_n - 1, frames_n)
    t_up, t_down = lax.rem(t_me + 1, tiles_n), lax.rem(t_me + tiles_n - 1, tiles_n)
    targets = (
        (f_me, t_down), (f_up, t_down), (f_down, t_down), (f_up, t_me), (f_down, t_me),
        (f_me, t_up), (f_up, t_up), (f_down, t_up),
    )
    barrier = pltpu.get_barrier_semaphore()
    for where in targets:
        pl.semaphore_signal(barrier, inc=1, device_id=where, device_id_type=MESH)

    low = lax.broadcasted_iota(jnp.int32, (4, 8, LANES), 1) < 4
    for f in range(4):
        rows = x_ref[f].astype(F32)
        rows = jnp.concatenate([rows, jnp.zeros((8, 32, LANES - C), F32)], 2).reshape(8, 4, 8, LANES)
        for p in range(4):
            a, b = rows[2 * p], rows[2 * p + 1]
            at = slice(8 * (p % 2), 8 * (p % 2) + 8)
            cells[f, p // 2, 0, :, at, :] = jnp.where(low, a, pltpu.roll(b, 4, 1))
            cells[f, p // 2, 1, :, at, :] = jnp.where(low, pltpu.roll(a, 4, 1), b)

    head = lax.broadcasted_iota(jnp.int32, (128, LANES), 1)
    for h in range(HEADS):
        inside = ((head >= h * HEAD) & (head < (h + 1) * HEAD)) | (head >= C)
        ones_s[h * 128 : (h + 1) * 128, :] = jnp.where(inside, 2.0**-3, 0.0).astype(BF)
    prepare_weights(0, qkv_ref, proj_ref, in_ref, out_ref, qkv_s, proj_s, in_s, out_s)

    def copies(n, lo, hi):
        pairs = (
            (normed.at[:, 0, :, lo:hi], next_t.at[1:5, :, lo:hi]),
            (normed.at[3, 0, :, lo:hi], next_t.at[0, :, lo:hi]),
            (normed.at[0, 0, :, lo:hi], next_t.at[5, :, lo:hi]),
            (normed.at[3, :, :, lo:hi], last_f.at[:, :, lo:hi]),
            (normed.at[0, :, :, lo:hi], next_f.at[:, :, lo:hi]),
            (normed.at[:, 1, :, lo:hi], last_t.at[1:5, :, lo:hi]),
            (normed.at[3, 1, :, lo:hi], last_t.at[0, :, lo:hi]),
            (normed.at[0, 1, :, lo:hi], last_t.at[5, :, lo:hi]),
        )
        return [
            pltpu.make_async_remote_copy(
                src_ref=s, dst_ref=d, send_sem=send.at[n, i], recv_sem=recv.at[n, i],
                device_id=targets[i], device_id_type=MESH,
            )
            for i, (s, d) in enumerate(pairs)
        ]

    sent = []
    for n, (lo, hi) in enumerate(FIRST_GROUPS):
        order = [
            (f, q, g, s)
            for s in range(lo, hi) for m in range(2)
            for f in (2 * m, 2 * m + 1) for q in range(2) for g in range(2)
        ]
        x = jnp.concatenate([cells[i] for i in order], 0)
        y = layer(x, qkv_s[0], proj_s[0], in_s[0], out_s[0], ones_s[...])
        z = norm_tokens(y.astype(F32))
        for j, i in enumerate(order):
            own[i] = y[16 * j : 16 * j + 16]
            normed[i] = z[16 * j : 16 * j + 16]
        if n == 0:
            pl.semaphore_wait(barrier, 8)
        sent.append(copies(n, lo, hi))
        for c in sent[-1]:
            c.start()

    r = lax.broadcasted_iota(jnp.int32, (256, 256), 0)
    c = lax.broadcasted_iota(jnp.int32, (256, 256), 1)
    start = (lax.rem(r, LANES) - C) * HEAD
    column = lax.rem(c, LANES)
    hits = (lax.rem(r, LANES) >= C) & (column >= start) & (column < start + HEAD) & (column < C)
    hits = hits & (r // LANES == c // LANES)
    spread_s[...] = jnp.where(hits, 1.0, 0.0).astype(BF)
    prepare_weights(1, qkv_ref, proj_ref, in_ref, out_ref, qkv_s, proj_s, in_s, out_s)

    def arrive(which):
        for group in sent:
            for i in which:
                group[i].wait_recv()

    columns = [((1, s), (0, (s + 1) % 4)) for s in range(4)]
    mine = [(f, j, s) for s in range(4) for f in range(4) for j in range(2)]
    wide = [(f, j, s) for s in range(4) for f in range(6) for j in range(2)]

    def beside(q, f, g, s):
        if f == 0:
            return last_f[q, g, s]
        return next_f[q, g, s] if f == 5 else normed[f - 1, q, g, s]

    def own_side(q):
        own_normed = jnp.concatenate([normed[(f, q) + columns[s][j]] for f, j, s in mine], 0)
        near = jnp.concatenate([beside(q, f, *columns[s][j]) for f, j, s in wide], 0)
        return second_queries(own_normed, qkv_s[1, :, 0:256]), second_keys(near, qkv_s[1, :, 256:768])

    def side(q, queries, near, halo):
        x = jnp.concatenate([own[(f, q) + columns[s][j]] for f, j, s in mine], 0).astype(F32)
        far = jnp.concatenate([halo[(f,) + columns[s][j]] for f, j, s in wide], 0)
        far = second_keys(far, qkv_s[1, :, 256:768])
        y = second_layer_side(
            x, queries, near, far, proj_s[1], in_s[1], out_s[1], spread_s[...]
        )
        for i, (f, j, s) in enumerate(mine):
            o_ref[f, q, j, s] = y[16 * i : 16 * i + 16]

    arrive((0, 1, 2, 3, 4))
    side(1, *own_side(1), next_t)
    early = own_side(0)
    arrive((5, 6, 7))
    side(0, *early, last_t)
    for group in sent:
        for c in group:
            c.wait_send()


def rows_out(cells_ref, o_ref):
    low = lax.broadcasted_iota(jnp.int32, (4, 8, LANES), 1) < 4
    for f in range(4):
        for q in range(2):
            right = cells_ref[f, q, 0].astype(F32)
            left = jnp.concatenate([cells_ref[f, q, 1, 3:4], cells_ref[f, q, 1, 0:3]], 0).astype(F32)
            for h in range(2):
                a, b = left[:, 8 * h : 8 * h + 8], right[:, 8 * h : 8 * h + 8]
                r = 4 * q + 2 * h
                even = jnp.where(low, a, pltpu.roll(b, 4, 1)).reshape(32, LANES)
                odd = jnp.where(low, pltpu.roll(a, 4, 1), b).reshape(32, LANES)
                o_ref[f, r] = even[:, :C].astype(BF)
                o_ref[f, r + 1] = odd[:, :C].astype(BF)


def local(frames_n, tiles_n, feats, qkv_weight, proj_weight, mlp_in, mlp_out):
    vmem = pl.BlockSpec(memory_space=pltpu.VMEM)
    halo = (2, 4, 16, LANES)
    restored = pl.pallas_call(
        functools.partial(kernel, frames_n, tiles_n),
        out_shape=pltpu.VMEM((4, 2) + halo, feats.dtype),
        in_specs=[vmem] * 5,
        out_specs=vmem,
        scratch_shapes=[
            pltpu.VMEM((2, 128, 768), BF),
            pltpu.VMEM((2, 256, 128), BF),
            pltpu.VMEM((2, 128, 512), BF),
            pltpu.VMEM((2, 256, 128), BF),
            pltpu.VMEM((768, 128), BF),
            pltpu.VMEM((256, 256), BF),
            pltpu.VMEM((4, 2) + halo, F32),
            pltpu.VMEM((4, 2) + halo, BF),
            pltpu.VMEM((4, 2) + halo, BF),
            pltpu.VMEM((6,) + halo, BF),
            pltpu.VMEM((6,) + halo, BF),
            pltpu.VMEM((2,) + halo, BF),
            pltpu.VMEM((2,) + halo, BF),
            pltpu.SemaphoreType.DMA((len(FIRST_GROUPS), 8)),
            pltpu.SemaphoreType.DMA((len(FIRST_GROUPS), 8)),
        ],
        compiler_params=pltpu.CompilerParams(
            collective_id=0, has_side_effects=True, vmem_limit_bytes=60 << 20
        ),
    )(feats, qkv_weight, proj_weight, mlp_in, mlp_out)
    return pl.pallas_call(
        rows_out,
        out_shape=jax.ShapeDtypeStruct(feats.shape, feats.dtype),
        in_specs=[vmem],
        out_specs=vmem,
    )(restored)


def solution(mesh):
    placed = (P("frame", "tile", None, None), P(), P(), P(), P())
    return jax.shard_map(
        functools.partial(local, mesh.shape["frame"], mesh.shape["tile"]),
        mesh=mesh, in_specs=placed, out_specs=P("frame", "tile", None, None), check_vma=False,
    )
```

```python
import functools

import jax
import jax.numpy as jnp
from jax import lax
from jax.experimental import pallas as pl
from jax.experimental.pallas import tpu as pltpu
from jax.sharding import PartitionSpec as P

C, HEADS, HEAD, HID = 120, 6, 20, 240
LANES = 128
EPSILON = 1e-05
LOG2E = 1.4426950408889634
MESH = pl.DeviceIdType.MESH
FIRST_GROUPS = ((0, 4),)
AHEAD = 2
BF, F32 = jnp.bfloat16, jnp.float32


def dot(a, b, dims=(((1,), (0,)), ((), ()))):
    return lax.dot_general(a, b, dims, preferred_element_type=F32)


def norm_tokens(x):
    mean = jnp.sum(x, -1, keepdims=True) * (1.0 / C)
    lane = lax.broadcasted_iota(jnp.int32, x.shape, 1)
    center = jnp.where(lane < C, x - mean, 0.0)
    spread = jnp.sum(center * center, -1, keepdims=True) * (1.0 / C)
    return (center * lax.rsqrt(spread + EPSILON)).astype(BF)


def gelu(g):
    return g * 0.5 * (1.0 + lax.erf(g * 0.7071067811865476))


def attend(q, k, v, key_masks, value_masks, ones):
    kb = jnp.concatenate([jnp.where(m, k, jnp.zeros_like(k)) for m in key_masks], 0)
    weights = jnp.exp2(dot(q, kb, (((1,), (1,)), ((), ())))).astype(BF)
    vb = jnp.concatenate([jnp.where(m, v, jnp.zeros_like(v)) for m in value_masks], 0)
    both = dot(weights, jnp.concatenate([vb, ones], 1))
    return both[:, :LANES] * (pl.reciprocal(both[:, LANES:], approx=False) * 16.0)


def layer(x, qkv_w, proj_w, in_w, out_w, ones):
    tokens = x.shape[0]
    packed = dot(norm_tokens(x), qkv_w)
    scaling = HEAD**-0.5 * LOG2E
    lane = lax.broadcasted_iota(jnp.int32, (tokens, LANES), 1)
    row = lax.broadcasted_iota(jnp.int32, (tokens, LANES), 0)
    hit = lane == C + lax.rem(row // 64, 2)
    self_q = (packed[:, 0:128] * scaling).astype(BF)
    self_k = packed[:, 128:256].astype(BF)
    self_v = (packed[:, 256:384] * 2.0**-7).astype(BF)
    mutual_q = jnp.where(hit, 1.0, packed[:, 384:512] * scaling).astype(BF)
    mutual_k = jnp.where(hit, -1e5, packed[:, 512:640]).astype(BF)
    mutual_v = (packed[:, 640:768] * 2.0**-7).astype(BF)
    one = lax.broadcasted_iota(jnp.int32, (128, LANES), 1)
    own = [(one >= h * HEAD) & (one < (h + 1) * HEAD) for h in range(HEADS)]
    own_spare = [m | (one >= C) for m in own]
    self_out, mutual_out = [], []
    for w in range(tokens // 128):
        a = slice(w * 128, (w + 1) * 128)
        self_out.append(attend(self_q[a], self_k[a], self_v[a], own, own, ones))
        mutual_out.append(attend(mutual_q[a], mutual_k[a], mutual_v[a], own_spare, own, ones))
    attended = jnp.concatenate(
        [jnp.concatenate(self_out, 0), jnp.concatenate(mutual_out, 0)], 1
    ).astype(BF)
    return finish(x, attended, proj_w, in_w, out_w)


def finish(x, attended, proj_w, in_w, out_w):
    middle = (x + dot(attended, proj_w)).astype(BF).astype(F32)
    widened = dot(norm_tokens(middle), in_w)
    gated = (gelu(widened[:, :256]) * widened[:, 256:]).astype(BF)
    return (middle + dot(gated, out_w)).astype(BF)


def side_by_side(a, b):
    zero = jnp.zeros_like(a)
    return jnp.concatenate([jnp.concatenate([a, zero], 1), jnp.concatenate([zero, b], 1)], 0)


def score_rows(q_self, q_mutual, k_self, k_mutual):
    one = lax.broadcasted_iota(jnp.int32, q_self.shape, 1)
    none = jnp.zeros_like(q_self)
    stack = []
    for h in range(HEADS):
        m = (one >= h * HEAD) & (one < (h + 1) * HEAD)
        parts = [jnp.where(m, q_self, none), jnp.where(m | (one >= C), q_mutual, none)]
        stack.append(jnp.concatenate(parts, 1))
    keys = side_by_side(k_self, k_mutual)
    return dot(jnp.concatenate(stack, 0), keys, (((1,), (1,)), ((), ())))


def weigh_rows(scores, v_self, v_mutual):
    both = dot(jnp.exp2(scores).astype(BF), side_by_side(v_self, v_mutual))
    n = scores.shape[0] // HEADS
    lane = lax.rem(lax.broadcasted_iota(jnp.int32, (n, 2 * LANES), 1), LANES)
    out = jnp.zeros((n, 2 * LANES), F32)
    for h in range(HEADS):
        keep = ((lane >= h * HEAD) & (lane < (h + 1) * HEAD)) | (lane == C + h)
        out = jnp.where(keep, both[h * n : (h + 1) * n], out)
    return out


def second_queries(own_normed, q_w):
    query = dot(own_normed, q_w) * (HEAD**-0.5 * LOG2E)
    lane = lax.broadcasted_iota(jnp.int32, (query.shape[0], LANES), 1)
    row = lax.broadcasted_iota(jnp.int32, (query.shape[0], LANES), 0)
    hit = lane == C + 1 - lax.rem(row // 32, 2)
    return query[:, :LANES].astype(BF), jnp.where(hit, 1.0, query[:, LANES:]).astype(BF)


def second_keys(normed, kv_w):
    packed = dot(normed, kv_w)
    lane = lax.broadcasted_iota(jnp.int32, (packed.shape[0], LANES), 1)
    row = lax.broadcasted_iota(jnp.int32, (packed.shape[0], LANES), 0)
    hit = lane == C + lax.rem(row // 32, 2)
    return (
        packed[:, 0:128].astype(BF),
        jnp.where(hit, -1e5, packed[:, 128:256]).astype(BF),
        jnp.where(lane >= C, 2.0**-3, packed[:, 256:384] * 2.0**-7).astype(BF),
        jnp.where(lane >= C, 2.0**-3, packed[:, 384:512] * 2.0**-7).astype(BF),
    )


def second_layer_side(x, queries, near, far, proj_w, in_w, out_w, spread):
    windows = []
    for s in range(x.shape[0] // 128):
        for first, last, pair in ((0, 32, 0), (32, 96, 1), (96, 128, 2)):
            b = slice(192 * s + 64 * pair, 192 * s + 64 * pair + 64)
            kv = [jnp.concatenate([n[b], f[b]], 0) for n, f in zip(near, far)]
            windows.append([q[128 * s + first : 128 * s + last] for q in queries] + kv)
    scores, sums = [], []
    for w in range(len(windows) + AHEAD):
        if w < len(windows):
            scores.append(score_rows(*windows[w][:4]))
        if w >= AHEAD:
            sums.append(weigh_rows(scores[w - AHEAD], *windows[w - AHEAD][4:]))
    sums = jnp.concatenate(sums, 0)
    lane = lax.rem(lax.broadcasted_iota(jnp.int32, sums.shape, 1), LANES)
    held = (lane >= C) & (lane < C + HEADS)
    inverse = jnp.where(held, pl.reciprocal(jnp.where(held, sums, 1.0), approx=False) * 16.0, 0.0)
    high = inverse.astype(BF)
    low = (inverse - high.astype(F32)).astype(BF)
    attended = (sums * (dot(high, spread) + dot(low, spread))).astype(BF)
    return finish(x, attended, proj_w, in_w, out_w)


def pad(w, rows, lanes):
    if lanes > w.shape[1]:
        w = jnp.concatenate([w, jnp.zeros((w.shape[0], lanes - w.shape[1]), w.dtype)], 1)
    if rows > w.shape[0]:
        w = jnp.concatenate([w, jnp.zeros((rows - w.shape[0], lanes), w.dtype)], 0)
    return w


def prepare_weights(l, qkv_ref, proj_ref, in_ref, out_ref, qkv_s, proj_s, in_s, out_s):
    w = qkv_ref[l].astype(F32)
    for i in range(6):
        part = pad(w[:, i * C : (i + 1) * C], LANES, LANES)
        at = i if l == 0 else (0, 2, 4, 1, 3, 5)[i]
        qkv_s[l, :, at * LANES : (at + 1) * LANES] = part.astype(BF)
    w = proj_ref[l].astype(F32)
    for i in range(2):
        proj_s[l, i * LANES : (i + 1) * LANES, :] = pad(w[i * C : (i + 1) * C], LANES, LANES).astype(BF)
    w = in_ref[l].astype(F32)
    for i in range(2):
        in_s[l, :, i * 256 : (i + 1) * 256] = pad(w[:, i * HID : (i + 1) * HID], LANES, 256).astype(BF)
    out_s[l] = pad(out_ref[l].astype(F32), 256, LANES).astype(BF)


def kernel(
    frames_n, tiles_n,
    x_ref, qkv_ref, proj_ref, in_ref, out_ref, o_ref,
    qkv_s, proj_s, in_s, out_s, ones_s, spread_s, cells, own, normed, next_t, last_t, last_f, next_f,
    send, recv,
):
    f_me, t_me = lax.axis_index("frame"), lax.axis_index("tile")
    f_up, f_down = lax.rem(f_me + 1, frames_n), lax.rem(f_me + frames_n - 1, frames_n)
    t_up, t_down = lax.rem(t_me + 1, tiles_n), lax.rem(t_me + tiles_n - 1, tiles_n)
    targets = (
        (f_me, t_down), (f_up, t_down), (f_down, t_down), (f_up, t_me), (f_down, t_me),
        (f_me, t_up), (f_up, t_up), (f_down, t_up),
    )
    barrier = pltpu.get_barrier_semaphore()
    for where in targets:
        pl.semaphore_signal(barrier, inc=1, device_id=where, device_id_type=MESH)

    low = lax.broadcasted_iota(jnp.int32, (4, 8, LANES), 1) < 4
    for f in range(4):
        rows = x_ref[f].astype(F32)
        rows = jnp.concatenate([rows, jnp.zeros((8, 32, LANES - C), F32)], 2).reshape(8, 4, 8, LANES)
        for p in range(4):
            a, b = rows[2 * p], rows[2 * p + 1]
            at = slice(8 * (p % 2), 8 * (p % 2) + 8)
            cells[f, p // 2, 0, :, at, :] = jnp.where(low, a, pltpu.roll(b, 4, 1))
            cells[f, p // 2, 1, :, at, :] = jnp.where(low, pltpu.roll(a, 4, 1), b)

    head = lax.broadcasted_iota(jnp.int32, (128, LANES), 1)
    for h in range(HEADS):
        inside = ((head >= h * HEAD) & (head < (h + 1) * HEAD)) | (head >= C)
        ones_s[h * 128 : (h + 1) * 128, :] = jnp.where(inside, 2.0**-3, 0.0).astype(BF)
    prepare_weights(0, qkv_ref, proj_ref, in_ref, out_ref, qkv_s, proj_s, in_s, out_s)

    def copies(n, lo, hi):
        pairs = (
            (normed.at[:, 0, :, lo:hi], next_t.at[1:5, :, lo:hi]),
            (normed.at[3, 0, :, lo:hi], next_t.at[0, :, lo:hi]),
            (normed.at[0, 0, :, lo:hi], next_t.at[5, :, lo:hi]),
            (normed.at[3, :, :, lo:hi], last_f.at[:, :, lo:hi]),
            (normed.at[0, :, :, lo:hi], next_f.at[:, :, lo:hi]),
            (normed.at[:, 1, :, lo:hi], last_t.at[1:5, :, lo:hi]),
            (normed.at[3, 1, :, lo:hi], last_t.at[0, :, lo:hi]),
            (normed.at[0, 1, :, lo:hi], last_t.at[5, :, lo:hi]),
        )
        return [
            pltpu.make_async_remote_copy(
                src_ref=s, dst_ref=d, send_sem=send.at[n, i], recv_sem=recv.at[n, i],
                device_id=targets[i], device_id_type=MESH,
            )
            for i, (s, d) in enumerate(pairs)
        ]

    sent = []
    for n, (lo, hi) in enumerate(FIRST_GROUPS):
        order = [
            (f, q, g, s)
            for s in range(lo, hi) for m in range(2)
            for f in (2 * m, 2 * m + 1) for q in range(2) for g in range(2)
        ]
        x = jnp.concatenate([cells[i] for i in order], 0)
        y = layer(x, qkv_s[0], proj_s[0], in_s[0], out_s[0], ones_s[...])
        z = norm_tokens(y.astype(F32))
        for j, i in enumerate(order):
            own[i] = y[16 * j : 16 * j + 16]
            normed[i] = z[16 * j : 16 * j + 16]
        if n == 0:
            pl.semaphore_wait(barrier, 8)
        sent.append(copies(n, lo, hi))
        for c in sent[-1]:
            c.start()

    r = lax.broadcasted_iota(jnp.int32, (256, 256), 0)
    c = lax.broadcasted_iota(jnp.int32, (256, 256), 1)
    start = (lax.rem(r, LANES) - C) * HEAD
    column = lax.rem(c, LANES)
    hits = (lax.rem(r, LANES) >= C) & (column >= start) & (column < start + HEAD) & (column < C)
    hits = hits & (r // LANES == c // LANES)
    spread_s[...] = jnp.where(hits, 1.0, 0.0).astype(BF)
    prepare_weights(1, qkv_ref, proj_ref, in_ref, out_ref, qkv_s, proj_s, in_s, out_s)

    def arrive(which):
        for group in sent:
            for i in which:
                group[i].wait_recv()

    columns = [((1, s), (0, (s + 1) % 4)) for s in range(4)]
    mine = [(f, j, s) for s in range(4) for f in range(4) for j in range(2)]
    wide = [(f, j, s) for s in range(4) for f in range(6) for j in range(2)]

    def beside(q, f, g, s):
        if f == 0:
            return last_f[q, g, s]
        return next_f[q, g, s] if f == 5 else normed[f - 1, q, g, s]

    def own_side(q):
        own_normed = jnp.concatenate([normed[(f, q) + columns[s][j]] for f, j, s in mine], 0)
        near = jnp.concatenate([beside(q, f, *columns[s][j]) for f, j, s in wide], 0)
        return second_queries(own_normed, qkv_s[1, :, 0:256]), second_keys(near, qkv_s[1, :, 256:768])

    def side(q, queries, near, halo):
        x = jnp.concatenate([own[(f, q) + columns[s][j]] for f, j, s in mine], 0).astype(F32)
        far = jnp.concatenate([halo[(f,) + columns[s][j]] for f, j, s in wide], 0)
        far = second_keys(far, qkv_s[1, :, 256:768])
        y = second_layer_side(
            x, queries, near, far, proj_s[1], in_s[1], out_s[1], spread_s[...]
        )
        for i, (f, j, s) in enumerate(mine):
            o_ref[f, q, j, s] = y[16 * i : 16 * i + 16]

    arrive((0, 1, 2, 3, 4))
    side(1, *own_side(1), next_t)
    early = own_side(0)
    arrive((5, 6, 7))
    side(0, *early, last_t)
    for group in sent:
        for c in group:
            c.wait_send()


def rows_out(cells_ref, o_ref):
    low = lax.broadcasted_iota(jnp.int32, (4, 8, LANES), 1) < 4
    for f in range(4):
        for q in range(2):
            right = cells_ref[f, q, 0].astype(F32)
            left = jnp.concatenate([cells_ref[f, q, 1, 3:4], cells_ref[f, q, 1, 0:3]], 0).astype(F32)
            for h in range(2):
                a, b = left[:, 8 * h : 8 * h + 8], right[:, 8 * h : 8 * h + 8]
                r = 4 * q + 2 * h
                even = jnp.where(low, a, pltpu.roll(b, 4, 1)).reshape(32, LANES)
                odd = jnp.where(low, pltpu.roll(a, 4, 1), b).reshape(32, LANES)
                o_ref[f, r] = even[:, :C].astype(BF)
                o_ref[f, r + 1] = odd[:, :C].astype(BF)


def local(frames_n, tiles_n, feats, qkv_weight, proj_weight, mlp_in, mlp_out):
    vmem = pl.BlockSpec(memory_space=pltpu.VMEM)
    halo = (2, 4, 16, LANES)
    restored = pl.pallas_call(
        functools.partial(kernel, frames_n, tiles_n),
        out_shape=pltpu.VMEM((4, 2) + halo, feats.dtype),
        in_specs=[vmem] * 5,
        out_specs=vmem,
        scratch_shapes=[
            pltpu.VMEM((2, 128, 768), BF),
            pltpu.VMEM((2, 256, 128), BF),
            pltpu.VMEM((2, 128, 512), BF),
            pltpu.VMEM((2, 256, 128), BF),
            pltpu.VMEM((768, 128), BF),
            pltpu.VMEM((256, 256), BF),
            pltpu.VMEM((4, 2) + halo, F32),
            pltpu.VMEM((4, 2) + halo, BF),
            pltpu.VMEM((4, 2) + halo, BF),
            pltpu.VMEM((6,) + halo, BF),
            pltpu.VMEM((6,) + halo, BF),
            pltpu.VMEM((2,) + halo, BF),
            pltpu.VMEM((2,) + halo, BF),
            pltpu.SemaphoreType.DMA((len(FIRST_GROUPS), 8)),
            pltpu.SemaphoreType.DMA((len(FIRST_GROUPS), 8)),
        ],
        compiler_params=pltpu.CompilerParams(
            collective_id=0, has_side_effects=True, vmem_limit_bytes=60 << 20
        ),
    )(feats, qkv_weight, proj_weight, mlp_in, mlp_out)
    return pl.pallas_call(
        rows_out,
        out_shape=jax.ShapeDtypeStruct(feats.shape, feats.dtype),
        in_specs=[vmem],
        out_specs=vmem,
        compiler_params=pltpu.CompilerParams(vmem_limit_bytes=4 << 20),
    )(restored)


def solution(mesh):
    placed = (P("frame", "tile", None, None), P(), P(), P(), P())
    return jax.shard_map(
        functools.partial(local, mesh.shape["frame"], mesh.shape["tile"]),
        mesh=mesh, in_specs=placed, out_specs=P("frame", "tile", None, None), check_vma=False,
    )
```

```python
import functools

import jax
import jax.numpy as jnp
from jax import lax
from jax.experimental import pallas as pl
from jax.experimental.pallas import tpu as pltpu
from jax.sharding import PartitionSpec as P

C, HEADS, HEAD, HID = 120, 6, 20, 240
LANES = 128
EPSILON = 1e-05
LOG2E = 1.4426950408889634
MESH = pl.DeviceIdType.MESH
FIRST_GROUPS = ((0, 4),)
AHEAD = 3
BF, F32 = jnp.bfloat16, jnp.float32


def dot(a, b, dims=(((1,), (0,)), ((), ()))):
    return lax.dot_general(a, b, dims, preferred_element_type=F32)


def norm_tokens(x):
    mean = jnp.sum(x, -1, keepdims=True) * (1.0 / C)
    lane = lax.broadcasted_iota(jnp.int32, x.shape, 1)
    center = jnp.where(lane < C, x - mean, 0.0)
    spread = jnp.sum(center * center, -1, keepdims=True) * (1.0 / C)
    return (center * lax.rsqrt(spread + EPSILON)).astype(BF)


def gelu(g):
    return g * 0.5 * (1.0 + lax.erf(g * 0.7071067811865476))


def attend(q, k, v, key_masks, value_masks, ones):
    kb = jnp.concatenate([jnp.where(m, k, jnp.zeros_like(k)) for m in key_masks], 0)
    weights = jnp.exp2(dot(q, kb, (((1,), (1,)), ((), ())))).astype(BF)
    vb = jnp.concatenate([jnp.where(m, v, jnp.zeros_like(v)) for m in value_masks], 0)
    both = dot(weights, jnp.concatenate([vb, ones], 1))
    return both[:, :LANES] * (pl.reciprocal(both[:, LANES:], approx=False) * 16.0)


def layer(x, qkv_w, proj_w, in_w, out_w, ones):
    tokens = x.shape[0]
    packed = dot(norm_tokens(x), qkv_w)
    scaling = HEAD**-0.5 * LOG2E
    lane = lax.broadcasted_iota(jnp.int32, (tokens, LANES), 1)
    row = lax.broadcasted_iota(jnp.int32, (tokens, LANES), 0)
    hit = lane == C + lax.rem(row // 64, 2)
    self_q = (packed[:, 0:128] * scaling).astype(BF)
    self_k = packed[:, 128:256].astype(BF)
    self_v = (packed[:, 256:384] * 2.0**-7).astype(BF)
    mutual_q = jnp.where(hit, 1.0, packed[:, 384:512] * scaling).astype(BF)
    mutual_k = jnp.where(hit, -1e5, packed[:, 512:640]).astype(BF)
    mutual_v = (packed[:, 640:768] * 2.0**-7).astype(BF)
    one = lax.broadcasted_iota(jnp.int32, (128, LANES), 1)
    own = [(one >= h * HEAD) & (one < (h + 1) * HEAD) for h in range(HEADS)]
    own_spare = [m | (one >= C) for m in own]
    self_out, mutual_out = [], []
    for w in range(tokens // 128):
        a = slice(w * 128, (w + 1) * 128)
        self_out.append(attend(self_q[a], self_k[a], self_v[a], own, own, ones))
        mutual_out.append(attend(mutual_q[a], mutual_k[a], mutual_v[a], own_spare, own, ones))
    attended = jnp.concatenate(
        [jnp.concatenate(self_out, 0), jnp.concatenate(mutual_out, 0)], 1
    ).astype(BF)
    return finish(x, attended, proj_w, in_w, out_w)


def finish(x, attended, proj_w, in_w, out_w):
    middle = (x + dot(attended, proj_w)).astype(BF).astype(F32)
    widened = dot(norm_tokens(middle), in_w)
    gated = (gelu(widened[:, :256]) * widened[:, 256:]).astype(BF)
    return (middle + dot(gated, out_w)).astype(BF)


def side_by_side(a, b):
    zero = jnp.zeros_like(a)
    return jnp.concatenate([jnp.concatenate([a, zero], 1), jnp.concatenate([zero, b], 1)], 0)


def score_rows(q_self, q_mutual, k_self, k_mutual):
    one = lax.broadcasted_iota(jnp.int32, q_self.shape, 1)
    none = jnp.zeros_like(q_self)
    stack = []
    for h in range(HEADS):
        m = (one >= h * HEAD) & (one < (h + 1) * HEAD)
        parts = [jnp.where(m, q_self, none), jnp.where(m | (one >= C), q_mutual, none)]
        stack.append(jnp.concatenate(parts, 1))
    keys = side_by_side(k_self, k_mutual)
    return dot(jnp.concatenate(stack, 0), keys, (((1,), (1,)), ((), ())))


def weigh_rows(scores, v_self, v_mutual):
    both = dot(jnp.exp2(scores).astype(BF), side_by_side(v_self, v_mutual))
    n = scores.shape[0] // HEADS
    lane = lax.rem(lax.broadcasted_iota(jnp.int32, (n, 2 * LANES), 1), LANES)
    out = jnp.zeros((n, 2 * LANES), F32)
    for h in range(HEADS):
        keep = ((lane >= h * HEAD) & (lane < (h + 1) * HEAD)) | (lane == C + h)
        out = jnp.where(keep, both[h * n : (h + 1) * n], out)
    return out


def second_queries(own_normed, q_w):
    query = dot(own_normed, q_w) * (HEAD**-0.5 * LOG2E)
    lane = lax.broadcasted_iota(jnp.int32, (query.shape[0], LANES), 1)
    row = lax.broadcasted_iota(jnp.int32, (query.shape[0], LANES), 0)
    hit = lane == C + 1 - lax.rem(row // 32, 2)
    return query[:, :LANES].astype(BF), jnp.where(hit, 1.0, query[:, LANES:]).astype(BF)


def second_keys(normed, kv_w):
    packed = dot(normed, kv_w)
    lane = lax.broadcasted_iota(jnp.int32, (packed.shape[0], LANES), 1)
    row = lax.broadcasted_iota(jnp.int32, (packed.shape[0], LANES), 0)
    hit = lane == C + lax.rem(row // 32, 2)
    return (
        packed[:, 0:128].astype(BF),
        jnp.where(hit, -1e5, packed[:, 128:256]).astype(BF),
        jnp.where(lane >= C, 2.0**-3, packed[:, 256:384] * 2.0**-7).astype(BF),
        jnp.where(lane >= C, 2.0**-3, packed[:, 384:512] * 2.0**-7).astype(BF),
    )


def second_layer_side(x, queries, near, far, proj_w, in_w, out_w, spread):
    windows = []
    for s in range(x.shape[0] // 128):
        for first, last, pair in ((0, 32, 0), (32, 96, 1), (96, 128, 2)):
            b = slice(192 * s + 64 * pair, 192 * s + 64 * pair + 64)
            kv = [jnp.concatenate([n[b], f[b]], 0) for n, f in zip(near, far)]
            windows.append([q[128 * s + first : 128 * s + last] for q in queries] + kv)
    scores, sums = [], []
    for w in range(len(windows) + AHEAD):
        if w < len(windows):
            scores.append(score_rows(*windows[w][:4]))
        if w >= AHEAD:
            sums.append(weigh_rows(scores[w - AHEAD], *windows[w - AHEAD][4:]))
    sums = jnp.concatenate(sums, 0)
    lane = lax.rem(lax.broadcasted_iota(jnp.int32, sums.shape, 1), LANES)
    held = (lane >= C) & (lane < C + HEADS)
    inverse = jnp.where(held, pl.reciprocal(jnp.where(held, sums, 1.0), approx=False) * 16.0, 0.0)
    high = inverse.astype(BF)
    low = (inverse - high.astype(F32)).astype(BF)
    attended = (sums * (dot(high, spread) + dot(low, spread))).astype(BF)
    return finish(x, attended, proj_w, in_w, out_w)


def pad(w, rows, lanes):
    if lanes > w.shape[1]:
        w = jnp.concatenate([w, jnp.zeros((w.shape[0], lanes - w.shape[1]), w.dtype)], 1)
    if rows > w.shape[0]:
        w = jnp.concatenate([w, jnp.zeros((rows - w.shape[0], lanes), w.dtype)], 0)
    return w


def prepare_weights(l, qkv_ref, proj_ref, in_ref, out_ref, qkv_s, proj_s, in_s, out_s):
    w = qkv_ref[l].astype(F32)
    for i in range(6):
        part = pad(w[:, i * C : (i + 1) * C], LANES, LANES)
        at = i if l == 0 else (0, 2, 4, 1, 3, 5)[i]
        qkv_s[l, :, at * LANES : (at + 1) * LANES] = part.astype(BF)
    w = proj_ref[l].astype(F32)
    for i in range(2):
        proj_s[l, i * LANES : (i + 1) * LANES, :] = pad(w[i * C : (i + 1) * C], LANES, LANES).astype(BF)
    w = in_ref[l].astype(F32)
    for i in range(2):
        in_s[l, :, i * 256 : (i + 1) * 256] = pad(w[:, i * HID : (i + 1) * HID], LANES, 256).astype(BF)
    out_s[l] = pad(out_ref[l].astype(F32), 256, LANES).astype(BF)


def kernel(
    frames_n, tiles_n,
    x_ref, qkv_ref, proj_ref, in_ref, out_ref, o_ref,
    qkv_s, proj_s, in_s, out_s, ones_s, spread_s, cells, own, normed, next_t, last_t, last_f, next_f,
    send, recv, raw_qkv, raw_proj, raw_in, raw_out, fetch,
):
    f_me, t_me = lax.axis_index("frame"), lax.axis_index("tile")
    f_up, f_down = lax.rem(f_me + 1, frames_n), lax.rem(f_me + frames_n - 1, frames_n)
    t_up, t_down = lax.rem(t_me + 1, tiles_n), lax.rem(t_me + tiles_n - 1, tiles_n)
    targets = (
        (f_me, t_down), (f_up, t_down), (f_down, t_down), (f_up, t_me), (f_down, t_me),
        (f_me, t_up), (f_up, t_up), (f_down, t_up),
    )
    stored = (qkv_ref, proj_ref, in_ref, out_ref)
    raw = (raw_qkv, raw_proj, raw_in, raw_out)
    fetched = [
        [pltpu.make_async_copy(a.at[l], b.at[l], fetch.at[l, i]) for i, (a, b) in enumerate(zip(stored, raw))]
        for l in range(2)
    ]
    for group in fetched:
        for c in group:
            c.start()
    barrier = pltpu.get_barrier_semaphore()
    for where in targets:
        pl.semaphore_signal(barrier, inc=1, device_id=where, device_id_type=MESH)

    low = lax.broadcasted_iota(jnp.int32, (4, 8, LANES), 1) < 4
    for f in range(4):
        rows = x_ref[f].astype(F32)
        rows = jnp.concatenate([rows, jnp.zeros((8, 32, LANES - C), F32)], 2).reshape(8, 4, 8, LANES)
        for p in range(4):
            a, b = rows[2 * p], rows[2 * p + 1]
            at = slice(8 * (p % 2), 8 * (p % 2) + 8)
            cells[f, p // 2, 0, :, at, :] = jnp.where(low, a, pltpu.roll(b, 4, 1))
            cells[f, p // 2, 1, :, at, :] = jnp.where(low, pltpu.roll(a, 4, 1), b)

    head = lax.broadcasted_iota(jnp.int32, (128, LANES), 1)
    for h in range(HEADS):
        inside = ((head >= h * HEAD) & (head < (h + 1) * HEAD)) | (head >= C)
        ones_s[h * 128 : (h + 1) * 128, :] = jnp.where(inside, 2.0**-3, 0.0).astype(BF)
    for c in fetched[0]:
        c.wait()
    prepare_weights(0, *raw, qkv_s, proj_s, in_s, out_s)

    def copies(n):
        pairs = (
            (normed.at[0], next_t.at[1:5]),
            (normed.at[0, 3], next_t.at[0]),
            (normed.at[0, 0], next_t.at[5]),
            (normed.at[:, 3], last_f),
            (normed.at[:, 0], next_f),
            (normed.at[1], last_t.at[1:5]),
            (normed.at[1, 3], last_t.at[0]),
            (normed.at[1, 0], last_t.at[5]),
        )
        return [
            pltpu.make_async_remote_copy(
                src_ref=s, dst_ref=d, send_sem=send.at[n, i], recv_sem=recv.at[n, i],
                device_id=targets[i], device_id_type=MESH,
            )
            for i, (s, d) in enumerate(pairs)
        ]

    sent = []
    for n, (lo, hi) in enumerate(FIRST_GROUPS):
        order = [
            (f, q, g, s)
            for s in range(lo, hi) for m in range(2)
            for f in (2 * m, 2 * m + 1) for q in range(2) for g in range(2)
        ]
        x = jnp.concatenate([cells[i] for i in order], 0)
        y = layer(x, qkv_s[0], proj_s[0], in_s[0], out_s[0], ones_s[...])
        z = norm_tokens(y.astype(F32))
        for j, i in enumerate(order):
            own[i] = y[16 * j : 16 * j + 16]
            normed[i[1], i[0], i[2], i[3]] = z[16 * j : 16 * j + 16]
        if n == 0:
            pl.semaphore_wait(barrier, 8)
        sent.append(copies(n))
        for c in sent[-1]:
            c.start()

    r = lax.broadcasted_iota(jnp.int32, (256, 256), 0)
    c = lax.broadcasted_iota(jnp.int32, (256, 256), 1)
    start = (lax.rem(r, LANES) - C) * HEAD
    column = lax.rem(c, LANES)
    hits = (lax.rem(r, LANES) >= C) & (column >= start) & (column < start + HEAD) & (column < C)
    hits = hits & (r // LANES == c // LANES)
    spread_s[...] = jnp.where(hits, 1.0, 0.0).astype(BF)
    for c in fetched[1]:
        c.wait()
    prepare_weights(1, *raw, qkv_s, proj_s, in_s, out_s)

    def arrive(which):
        for group in sent:
            for i in which:
                group[i].wait_recv()

    columns = [((1, s), (0, (s + 1) % 4)) for s in range(4)]
    mine = [(f, j, s) for s in range(4) for f in range(4) for j in range(2)]
    wide = [(f, j, s) for s in range(4) for f in range(6) for j in range(2)]

    def beside(q, f, g, s):
        if f == 0:
            return last_f[q, g, s]
        return next_f[q, g, s] if f == 5 else normed[q, f - 1, g, s]

    def own_side(q):
        own_normed = jnp.concatenate([normed[(q, f) + columns[s][j]] for f, j, s in mine], 0)
        near = jnp.concatenate([beside(q, f, *columns[s][j]) for f, j, s in wide], 0)
        return second_queries(own_normed, qkv_s[1, :, 0:256]), second_keys(near, qkv_s[1, :, 256:768])

    def side(q, queries, near, halo):
        x = jnp.concatenate([own[(f, q) + columns[s][j]] for f, j, s in mine], 0).astype(F32)
        far = jnp.concatenate([halo[(f,) + columns[s][j]] for f, j, s in wide], 0)
        far = second_keys(far, qkv_s[1, :, 256:768])
        y = second_layer_side(
            x, queries, near, far, proj_s[1], in_s[1], out_s[1], spread_s[...]
        )
        for i, (f, j, s) in enumerate(mine):
            o_ref[f, q, j, s] = y[16 * i : 16 * i + 16]

    arrive((0, 1, 2, 3, 4))
    side(1, *own_side(1), next_t)
    early = own_side(0)
    arrive((5, 6, 7))
    side(0, *early, last_t)
    for group in sent:
        for c in group:
            c.wait_send()


def rows_out(cells_ref, o_ref):
    low = lax.broadcasted_iota(jnp.int32, (4, 8, LANES), 1) < 4
    for f in range(4):
        for q in range(2):
            right = cells_ref[f, q, 0].astype(F32)
            left = jnp.concatenate([cells_ref[f, q, 1, 3:4], cells_ref[f, q, 1, 0:3]], 0).astype(F32)
            for h in range(2):
                a, b = left[:, 8 * h : 8 * h + 8], right[:, 8 * h : 8 * h + 8]
                r = 4 * q + 2 * h
                even = jnp.where(low, a, pltpu.roll(b, 4, 1)).reshape(32, LANES)
                odd = jnp.where(low, pltpu.roll(a, 4, 1), b).reshape(32, LANES)
                o_ref[f, r] = even[:, :C].astype(BF)
                o_ref[f, r + 1] = odd[:, :C].astype(BF)


def local(frames_n, tiles_n, feats, qkv_weight, proj_weight, mlp_in, mlp_out):
    vmem = pl.BlockSpec(memory_space=pltpu.VMEM)
    halo = (2, 4, 16, LANES)
    restored = pl.pallas_call(
        functools.partial(kernel, frames_n, tiles_n),
        out_shape=pltpu.VMEM((4, 2) + halo, feats.dtype),
        in_specs=[vmem] + [pl.BlockSpec(memory_space=pl.ANY)] * 4,
        out_specs=vmem,
        scratch_shapes=[
            pltpu.VMEM((2, 128, 768), BF),
            pltpu.VMEM((2, 256, 128), BF),
            pltpu.VMEM((2, 128, 512), BF),
            pltpu.VMEM((2, 256, 128), BF),
            pltpu.VMEM((768, 128), BF),
            pltpu.VMEM((256, 256), BF),
            pltpu.VMEM((4, 2) + halo, F32),
            pltpu.VMEM((4, 2) + halo, BF),
            pltpu.VMEM((2, 4) + halo, BF),
            pltpu.VMEM((6,) + halo, BF),
            pltpu.VMEM((6,) + halo, BF),
            pltpu.VMEM((2,) + halo, BF),
            pltpu.VMEM((2,) + halo, BF),
            pltpu.SemaphoreType.DMA((len(FIRST_GROUPS), 8)),
            pltpu.SemaphoreType.DMA((len(FIRST_GROUPS), 8)),
            pltpu.VMEM(qkv_weight.shape, BF),
            pltpu.VMEM(proj_weight.shape, BF),
            pltpu.VMEM(mlp_in.shape, BF),
            pltpu.VMEM(mlp_out.shape, BF),
            pltpu.SemaphoreType.DMA((2, 4)),
        ],
        compiler_params=pltpu.CompilerParams(
            collective_id=0, has_side_effects=True, vmem_limit_bytes=60 << 20
        ),
    )(feats, qkv_weight, proj_weight, mlp_in, mlp_out)
    return pl.pallas_call(
        rows_out,
        out_shape=jax.ShapeDtypeStruct(feats.shape, feats.dtype),
        in_specs=[vmem],
        out_specs=vmem,
        compiler_params=pltpu.CompilerParams(vmem_limit_bytes=4 << 20),
    )(restored)


def solution(mesh):
    placed = (P("frame", "tile", None, None), P(), P(), P(), P())
    return jax.shard_map(
        functools.partial(local, mesh.shape["frame"], mesh.shape["tile"]),
        mesh=mesh, in_specs=placed, out_specs=P("frame", "tile", None, None), check_vma=False,
    )
```
